128 devices in a mesh: row: 8 (over z, core), col: 16 (over y, x).
Axes of the slice: x: 4, y: 4, z: 4, core: 2. Of those that a mesh axis runs over, the one named last changes fastest.
Arguments:
- diag_tile: float32 [512, 512], P(('row', 'col')), may hold values from -1 to 2
- pivot_order: int32 [512], replicated, may hold values from 0 to 511, as said below
- panel_col: bfloat16 [64, 512, 512], P('row', 'col'), may hold values from -0.25 to 0.25
- panel_row: bfloat16 [64, 2, 64, 512], P('col', None, None, 'row'), may hold values from -5 to 5
- trail_factors: bfloat16 [64, 64, 2, 64, 512], P('row', 'col'), may hold values from -5 to 5
- tile_ranks: int32 [64, 64], P('row', 'col'), may hold values from 1 to 64
- pattern: int32 [64], P('col'), may hold values 0 or 1
- near_vals: bfloat16 [32768, 512], P(('row', 'col')), may hold values from -0.75 to 0.75
- near_dest: int32 [32768, 1], P(('row', 'col')), may hold values from 0 to 127; in each aligned block of 256 rows (0 to 255, 256 to 511, ...) at most 4 rows name the same one
- near_row: int32 [32768], P(('row', 'col')), may hold values from 0 to 255
- near_count: int32 [128], P(('row', 'col')), may hold values from 1 to 256, 16384 in all
Outputs:
- updated: bfloat16 [64, 64, 512, 512], P('row', 'col')
The draws below stay inside these ranges and needn't reach their ends.
Inputs may be any that keep to these rules, and one draw needn't show every extreme that they name: `pivot_order`: a permutation of 0 to 511. `near_dest`: among the 256 slots of one device no device is named more than 4 times, and some device exactly 4 times. `near_count`: some partition has all 256 slots live.
All inputs are finite; a program needn't handle non-finite values. No bound on the sum of `pattern` or of `near_count` on one device may be relied on, other than what follows from the above.
Results may differ from the reference program's by a relative error of at most 0.0055.
Values may be sent and summed in bfloat16 or wider, within the bound.
A program may use at most 128 MiB of HBM per device.

```python
import math
import jax
import jax.numpy as jnp
import numpy as np
from jax import lax

B = 512
K = 64
TR = 8
NEAR = 256
NTR = 64
NTC = 64
RB = 32
PANEL_ROWS = 256
CAP = 4
N_ROW = 8
N_COL = 16


def shared_order(key):
    return jax.random.permutation(key, B).astype(jnp.int32)


def draw_pivot_order(key, part):
    return shared_order(key)


def draw_diag_tile(key, part):
    row_order = shared_order(key)
    key = jax.random.fold_in(key, 5)
    key_diag, key_noise = jax.random.split(key)
    diagonal = jax.random.uniform(key_diag, (B,), jnp.float32, 1.0, 2.0)
    noise = jax.random.truncated_normal(key_noise, -4.0, 4.0, (B, B), jnp.float32) * (0.3 / math.sqrt(B))
    identity = jnp.eye(B, dtype=jnp.float32)
    dominant = noise * (1.0 - identity) + identity * diagonal[None, :]
    return jnp.zeros((B, B), jnp.float32).at[row_order].set(dominant)


def set_ends(result, key, smallest, high):
    place = [jax.random.randint(jax.random.fold_in(key, axis), (), 0, length) for axis, length in enumerate(result.shape)]
    longest = result.shape.index(max(result.shape))
    beside = place[:longest] + [(place[longest] + 1) % result.shape[longest]] + place[longest + 1:]
    return result.at[tuple(place)].set(smallest).at[tuple(beside)].set(high)


def level_of(key, shape, cuts, least, top_value):
    def one(dim, parts):
        steps = jax.random.uniform(jax.random.fold_in(jax.random.fold_in(key, 6), dim), (parts,), jnp.float32, least / len(cuts), top_value / len(cuts))
        return jnp.repeat(jnp.exp(steps), shape[dim] // parts).reshape((-1,) + (1,) * (len(shape) - dim - 1))

    level = one(*cuts[0])
    for cut in cuts[1:]:
        level = level * one(*cut)
    return level


def split_up(count, total, most, lean):
    portions = [(1 << 20) // math.isqrt(rank ** lean) + 1 for rank in range(2, count + 1)]
    rest, given = total - most - (count - 1), [1] * (count - 1)
    while rest > 0:
        free = [i for i in range(count - 1) if given[i] < most]
        pool, remaining = sum([portions[i] for i in free]), rest
        for i in free:
            extra = min(most - given[i], max(1, remaining * portions[i] // pool), rest)
            given[i] = given[i] + extra
            rest = rest - extra
    return np.array([most] + given)


def uneven(own_key, count, total, limit, slope):
    if count == 2:
        one = jax.random.randint(own_key, (), max(1, total - limit), min(limit, total - 1) + 1)
        return jnp.stack([one, total - one])
    tallies = jnp.asarray(split_up(count, total, limit, slope), jnp.int32)
    twos = (count - 1) // 2
    giver, sink = tallies[1:1 + 2 * twos:2], tallies[2:2 + 2 * twos:2]
    margin = jnp.minimum(giver - 1, limit - sink)
    moved = jax.random.randint(jax.random.fold_in(own_key, 1), (twos,), 0, 1 << 20) % (margin + 1)
    tallies = tallies.at[1:1 + 2 * twos:2].set(giver - moved).at[2:2 + 2 * twos:2].set(sink + moved)
    return tallies[jax.random.permutation(jax.random.fold_in(own_key, 2), count)]


def shared_out(stream_key, own, number, rows, amount, top, most, lean):
    sequence = jax.random.permutation(stream_key, amount)
    crowded, usual = load_shares(amount, rows * top, most, lean, True), load_shares(amount, rows * top, most, lean, False)
    places = jnp.arange(amount)

    def named(sizes, turn):
        used = int((sizes > 0).sum())
        fixed = max(1, used // 4)
        passed = fixed + (places - fixed + turn * (used - fixed)) % max(1, amount - fixed)
        return jnp.zeros((amount,), jnp.int32).at[sequence[jnp.where(places < fixed, places, passed)]].set(jnp.asarray(sizes, jnp.int32))

    sizes = jnp.where(number % 4 == 0, named(crowded, number // 4), named(usual, number - number // 4 - 1))
    mixed = jax.random.permutation(jax.random.fold_in(own, 3), amount)
    giver, taker = mixed[0:amount // 2 * 2:2], mixed[1:amount // 2 * 2:2]
    slack = jnp.minimum(sizes[giver] - 1, most - sizes[taker]) // 2
    slack = jnp.where((giver == sequence[0]) | (taker == sequence[0]) | (sizes[taker] == 0), 0, jnp.maximum(slack, 0))
    passed = jax.random.randint(jax.random.fold_in(own, 4), (amount // 2,), 0, 1 << 20) % (slack + 1)
    sizes = sizes.at[giver].add(-passed).at[taker].add(passed)
    members = jnp.searchsorted(jnp.cumsum(sizes), jnp.arange(rows * top), side="right").astype(jnp.int32)
    grid = members.reshape(top, rows).T
    grid = grid[jax.random.permutation(jax.random.fold_in(own, 1), rows)]
    turn = jax.random.randint(jax.random.fold_in(own, 2), (rows, 1), 0, top)
    return jnp.take_along_axis(grid, (jnp.arange(top)[None, :] + turn) % top, axis=1)


def load_shares(number_of, total, limit, lean, full):
    portions = [(1 << 20) // math.isqrt(grade ** lean) + 1 for grade in range(1, number_of + 1)]
    largest = limit if full else min(limit, max(-(-total // number_of), total * portions[0] // sum(portions)))
    least = 1 if total - largest >= number_of - 1 else 0
    given, surplus = [largest] + [least] * (number_of - 1), total - largest - least * (number_of - 1)
    while surplus > 0:
        movable = [i for i in range(1, number_of) if given[i] < largest] or [i for i in range(1, number_of) if given[i] < limit]
        mass, remaining = sum([portions[i] for i in movable]), surplus
        for i in movable:
            more = min(limit - given[i], max(1, remaining * portions[i] // mass), surplus)
            given[i] = given[i] + more
            surplus = surplus - more
    return np.array(given)


def centred(rng, shape, spread, limit, cuts=(), held_as=jnp.bfloat16):
    entries = jax.random.normal(rng, shape, jnp.float32) * spread
    if len(cuts) > 0:
        entries = level_of(rng, shape, cuts, -0.22, 0.18) * entries
    return jnp.clip(entries, min=-limit, max=limit).astype(held_as)


def setup_inputs(seed: int = 0) -> dict:
    arg_keys = jax.random.split(jax.random.key(seed), 12)
    diag_tile = draw_diag_tile(jax.random.fold_in(arg_keys[11], 71), 0)
    pivot_order = draw_pivot_order(jax.random.fold_in(arg_keys[11], 71), 0)
    panel_col = centred(arg_keys[2], (NTR, B, B), B ** -0.5, 0.25, ((0, 8), (1, 16)))
    panel_row = centred(arg_keys[3], (NTC, 2, K, B), 0.35, 5.0, ((0, 16), (3, 8)))
    trail_factors = centred(arg_keys[4], (NTR, NTC, 2, K, B), 0.35, 5.0, ((0, 8), (1, 16)))
    tile_ranks = set_ends(jax.random.randint(arg_keys[5], (NTR, NTC), 1, K + 1), jax.random.fold_in(arg_keys[5], 1), 1, K).astype(jnp.int32)
    pattern = set_ends((jax.random.randint(arg_keys[6], (NTC,), 0, 4) < 3).astype(jnp.int32), jax.random.fold_in(arg_keys[6], 1), 0, 1)
    near_vals = centred(arg_keys[7], (N_ROW * N_COL * NEAR, B), 0.05, 0.75, ((0, 128),))
    near_dest_keys = jax.random.split(jax.random.fold_in(arg_keys[8], 1), (N_ROW * N_COL * NEAR) // NEAR)
    near_dest_turns = jax.random.permutation(jax.random.fold_in(arg_keys[8], 3), (N_ROW * N_COL * NEAR) // NEAR)
    near_dest = jax.vmap(lambda own, number: shared_out(jax.random.fold_in(arg_keys[8], 2), own, number, NEAR, N_ROW * N_COL, 1, CAP, 2))(near_dest_keys, near_dest_turns).reshape((N_ROW * N_COL * NEAR, 1))
    near_row = set_ends(jax.random.randint(arg_keys[9], (N_ROW * N_COL * NEAR,), 0, PANEL_ROWS), jax.random.fold_in(arg_keys[9], 1), 0, PANEL_ROWS - 1).astype(jnp.int32)
    near_count = uneven(arg_keys[10], N_ROW * N_COL, N_ROW * N_COL * NEAR // 2, NEAR, 1).astype(jnp.int32)
    return {"diag_tile": diag_tile, "pivot_order": pivot_order, "panel_col": panel_col, "panel_row": panel_row, "trail_factors": trail_factors, "tile_ranks": tile_ranks, "pattern": pattern, "near_vals": near_vals, "near_dest": near_dest, "near_row": near_row, "near_count": near_count}


highest_precision = lax.Precision.HIGHEST


def approximate_inverse(pivot_block):
    inverse = jnp.diag(1.0 / jnp.diagonal(pivot_block))
    for repeat in range(2):
        inner = jnp.dot(pivot_block, inverse, precision=highest_precision)
        inverse = 2.0 * inverse - jnp.dot(inverse, inner, precision=highest_precision)
    return inverse


def reference(diag_tile, pivot_order, panel_col, panel_row, trail_factors, tile_ranks, pattern, near_vals, near_dest, near_row, near_count):
    total_slots = N_ROW * N_COL * NEAR
    slot_ids = jnp.arange(total_slots, dtype=jnp.int32)
    owners = slot_ids // NEAR
    is_live = (slot_ids % NEAR) < near_count[owners]
    target_dev = near_dest[:, 0]
    tile_index = (target_dev // N_COL) * TR + near_row // RB
    row_index = (target_dev % N_COL) * RB + near_row % RB
    weights = near_vals.astype(jnp.float32) * is_live[:, None].astype(jnp.float32)
    corrections = jnp.zeros((NTR, B, B), jnp.float32).at[tile_index, row_index].add(weights)
    corrected = (panel_col.astype(jnp.float32) + corrections).astype(jnp.bfloat16)
    pivot_block = diag_tile[pivot_order]
    inverse = approximate_inverse(pivot_block)
    leading = panel_row[:, 0][:, :, pivot_order].astype(jnp.float32) * pattern[:, None, None].astype(jnp.float32)
    images = jnp.einsum("bc,jkc->jbk", inverse, leading, precision=highest_precision).astype(jnp.bfloat16)
    column_factors = panel_row[:, 1].astype(jnp.float32)

    def tile_row(operands):
        panel_tile, factor_row, rank_row = operands
        products = jnp.einsum("bc,jck->jbk", panel_tile.astype(jnp.float32), images.astype(jnp.float32)).astype(jnp.bfloat16)
        rank_mask = jnp.arange(K, dtype=jnp.int32)[None, :] < rank_row[:, None]
        left_masked = jnp.where(rank_mask[:, :, None], factor_row[:, 0].astype(jnp.float32), jnp.zeros((), jnp.float32))
        lowrank = jnp.einsum("jkb,jkc->jbc", left_masked, factor_row[:, 1].astype(jnp.float32))
        change = jnp.einsum("jbk,jkc->jbc", products.astype(jnp.float32), column_factors)
        return (lowrank - change).astype(jnp.bfloat16)

    return lax.map(tile_row, (corrected, trail_factors, tile_ranks))
```

```python
import jax
import jax.numpy as jnp
from jax import lax
from jax.experimental import pallas as pl
from jax.experimental.pallas import tpu as pltpu
from jax.sharding import PartitionSpec as P

B = 512
K = 64
TR = 8
TC = 4
NEAR = 256
CAP = 4
RB = 32
N_ROW = 8
N_COL = 16
N_DEV = 128
MESH = pl.DeviceIdType.MESH
F32 = jnp.float32
BF16 = jnp.bfloat16
NN = (((1,), (0,)), ((), ()))
NT = (((1,), (1,)), ((), ()))
TN = (((0,), (0,)), ((), ()))


def dot(a, b, dims):
    return lax.dot_general(a, b, dims, preferred_element_type=F32)


def iota(shape, dim):
    return lax.broadcasted_iota(jnp.int32, shape, dim)


def split(a):
    high = a.astype(BF16)
    return high, (a - high.astype(F32)).astype(BF16)


def halves_dot(a, b_high, b_low, dims):
    a_high, a_low = split(a)
    return dot(a_high, b_high, dims) + (dot(a_high, b_low, dims) + dot(a_low, b_high, dims))


def exchange_kernel(
    near_vals,
    near_dest,
    near_row,
    near_count,
    panel_col,
    diag_tile,
    pivot_order,
    panel_row,
    pattern,
    products,
    neg_v,
    near_out,
    near_in,
    meta_own,
    meta_row,
    meta_all,
    diag_x,
    diag_all,
    panel_all,
    grid,
    one_send,
    one_recv,
    ring_send,
    ring_recv,
):
    row = lax.axis_index("row")
    col = lax.axis_index("col")
    y, x = col // 4, lax.rem(col, 4)
    z, core = row // 2, lax.rem(row, 2)
    me = row * N_COL + col
    me_in = col * N_ROW + row

    def up(v):
        return lax.rem(v + 1, 4)

    def down(v):
        return lax.rem(v + 3, 4)

    barrier = pltpu.get_barrier_semaphore()

    def greet(step, carry):
        other = lax.rem(me + step, N_DEV)
        pl.semaphore_signal(
            barrier, inc=1, device_id=(other // N_COL, lax.rem(other, N_COL)), device_id_type=MESH
        )
        return carry

    lax.fori_loop(1, N_DEV, greet, 0)

    def copy(src, dst, sems, device):
        return pltpu.make_async_remote_copy(
            src_ref=src,
            dst_ref=dst,
            send_sem=sems[0],
            recv_sem=sems[1],
            device_id=device,
            device_id_type=MESH,
        )

    dest_col = near_dest[...]
    eye = iota((NEAR, NEAR), 0) == iota((NEAR, NEAR), 1)
    dest_lane = jnp.sum(jnp.where(eye, dest_col, 0), axis=0, keepdims=True)
    row_col = jnp.sum(jnp.where(eye, near_row[...], 0), axis=1, keepdims=True)
    earlier = (dest_col == dest_lane) & (iota((NEAR, NEAR), 1) < iota((NEAR, NEAR), 0))
    position = jnp.sum(jnp.where(earlier, 1, 0), axis=1, keepdims=True)
    live = iota((NEAR, 1), 0) < near_count[0]
    slot = jnp.where(live, dest_col * CAP + position, -1)
    placing = slot == iota((NEAR, N_DEV * CAP), 1)
    table = jnp.sum(jnp.where(placing, (row_col + 1).astype(F32), 0.0), axis=0, keepdims=True)
    placed = dot(jnp.where(placing, 1.0, 0.0).astype(BF16), near_vals[...], TN)
    low = iota((64, 8, 128), 1) < 4
    pieces = [placed[:, 128 * b : 128 * b + 128].reshape(64, 8, 128) for b in range(4)]
    turned = [pltpu.roll(p, 4, 1) for p in pieces]
    even = jnp.concatenate(
        [jnp.where(low, pieces[0], turned[1]), jnp.where(low, pieces[2], turned[3])], axis=1
    )
    odd = jnp.concatenate(
        [jnp.where(low, turned[0], pieces[1]), jnp.where(low, turned[2], pieces[3])], axis=1
    )
    both = jnp.concatenate([even[:, None], odd[:, None]], axis=1)
    near_out[...] = both.reshape(N_DEV, 16, 128).astype(BF16)

    meta = jnp.zeros((32, 128), F32)
    for m in range(4):
        meta = meta + jnp.where(
            iota((32, 128), 0) == 4 * row + m, table[:, 128 * m : 128 * m + 128], 0.0
        )
    meta_own[...] = meta.astype(BF16)

    own_rows = diag_tile[...]
    diag_x[x] = jnp.where(
        iota((16, B), 0) // 4 == x, jnp.concatenate([own_rows] * 4, axis=0), 0.0
    )
    panel_all[z, core] = panel_row[...]

    pl.semaphore_wait(barrier, N_DEV - 1)

    ones = iter(range(64))

    def sems():
        k = next(ones)
        return one_send.at[k], one_recv.at[k]

    def finish(copies):
        for c in copies:
            c.wait_recv()

    started = []

    def begin(copies):
        for c in copies:
            c.start()
        started.extend(copies)

    meta_row_copies = []
    for k in range(1, N_ROW):
        meta_row_copies.append(
            copy(meta_own, meta_row.at[k], sems(), (lax.rem(row + k, N_ROW), col))
        )
    begin(meta_row_copies)
    diag_x_copies = [
        copy(diag_x.at[x], diag_x.at[x], sems(), (row, 4 * y + lax.rem(x + k, 4))) for k in (1, 3, 2)
    ]
    begin(diag_x_copies)

    near_sems = sems()

    def send_near(step, carry):
        other = lax.rem(me + step, N_DEV)
        copy(
            near_out.at[other],
            near_in.at[me_in],
            near_sems,
            (other // N_COL, lax.rem(other, N_COL)),
        ).start()
        return carry

    lax.fori_loop(1, N_DEV, send_near, 0)
    near_in[me_in] = near_out[me]

    finish(meta_row_copies)
    total = meta_own[...].astype(F32)
    for k in range(1, N_ROW):
        total = total + meta_row[k].astype(F32)
    meta_all[col] = total.astype(BF16)
    meta_copies = [
        copy(meta_all.at[col], meta_all.at[col], sems(), (row, lax.rem(col + k, N_COL)))
        for k in range(1, N_COL)
    ]
    begin(meta_copies)

    finish(diag_x_copies)
    mine = diag_all.at[z, core, pl.ds(pl.multiple_of(16 * y, 16), 16)]
    mine[...] = (diag_x[0] + diag_x[1]) + (diag_x[2] + diag_x[3])
    diag_y_copies = [copy(mine, mine, sems(), (row, 4 * lax.rem(y + k, 4) + x)) for k in (1, 3, 2)]
    begin(diag_y_copies)

    panel_z_copies = [
        copy(
            panel_all.at[z, core],
            panel_all.at[z, core],
            sems(),
            (2 * lax.rem(z + k, 4) + core, col),
        )
        for k in (1, 3, 2)
    ]
    begin(panel_z_copies)

    wide_eye = iota((B, B), 0) == iota((B, B), 1)
    pivot_col = jnp.sum(jnp.where(wide_eye, pivot_order[...], 0), axis=1, keepdims=True)
    pivoting = jnp.where(pivot_col == iota((B, B), 1), 1.0, 0.0).astype(BF16)

    finish(meta_copies)
    slots = N_DEV * CAP
    ids = iota((slots, 1), 0)
    wanted = (ids // CAP) * CAP + me // 32
    choose = jnp.where(iota((slots, slots), 1) == wanted, 1.0, 0.0).astype(BF16)
    named = dot(choose, meta_all[...].reshape(slots, 128), NN)
    lane = lax.rem(me, 32) * CAP + lax.rem(ids, CAP)
    target = jnp.sum(jnp.where(iota((slots, 128), 1) == lane, named, 0.0), axis=1, keepdims=True)
    landing = jnp.where(target.astype(jnp.int32) - 1 == iota((slots, 256), 1), 1.0, 0.0).astype(BF16)

    finish(diag_y_copies)
    diag_z_copies = [
        copy(
            diag_all.at[z, core],
            diag_all.at[z, core],
            sems(),
            (2 * lax.rem(z + k, 4) + core, col),
        )
        for k in (1, 3, 2)
    ]
    begin(diag_z_copies)

    near_all = near_in.at[pl.ds(0, N_DEV - 1)]
    pltpu.make_async_copy(near_all, near_all, near_sems[1]).wait()
    both = near_in[...].astype(F32).reshape(64, 2, 16, 128)
    even, odd = both[:, 0], both[:, 1]
    columns = []
    for b in range(0, 4, 2):
        first, second = even[:, 4 * b : 4 * b + 8], odd[:, 4 * b : 4 * b + 8]
        columns.append(jnp.where(low, first, pltpu.roll(second, 4, 1)).reshape(slots, 128))
        columns.append(jnp.where(low, pltpu.roll(first, 4, 1), second).reshape(slots, 128))
    arrived = jnp.concatenate(columns, axis=1).astype(BF16)
    additions = dot(landing, arrived, TN)
    corrected = (panel_col[...].astype(F32) + additions.reshape(TR, RB, B)).astype(BF16)
    for i in range(TR):
        grid[i, y, x] = corrected[i]

    def ring_copy(i, phase, k, part, device):
        return copy(part, part, (ring_send.at[i, phase, k], ring_recv.at[i, phase, k]), device)

    def first_phase(i):
        if i % 2 == 0:
            plus, minus = (row, 4 * y + up(x)), (row, 4 * y + down(x))
            before, after = grid.at[i, y, down(x)], grid.at[i, y, up(x)]
        else:
            plus, minus = (row, 4 * up(y) + x), (row, 4 * down(y) + x)
            before, after = grid.at[i, down(y), x], grid.at[i, up(y), x]
        own = grid.at[i, y, x]
        return (
            ring_copy(i, 0, 0, own, plus),
            ring_copy(i, 0, 1, own, minus),
            ring_copy(i, 0, 2, before.at[pl.ds(0, 16)], plus),
            ring_copy(i, 0, 3, after.at[pl.ds(16, 16)], minus),
        )

    def second_phase(i):
        if i % 2 == 0:
            plus, minus = (row, 4 * up(y) + x), (row, 4 * down(y) + x)
            own = grid.at[i, y]
            before, after = grid.at[i, down(y), pl.ds(0, 2)], grid.at[i, up(y), pl.ds(2, 2)]
        else:
            plus, minus = (row, 4 * y + up(x)), (row, 4 * y + down(x))
            own = grid.at[i, :, x]
            before, after = grid.at[i, pl.ds(0, 2), down(x)], grid.at[i, pl.ds(2, 2), up(x)]
        return (
            ring_copy(i, 1, 0, own, plus),
            ring_copy(i, 1, 1, own, minus),
            ring_copy(i, 1, 2, before, plus),
            ring_copy(i, 1, 3, after, minus),
        )

    one = [first_phase(i) for i in range(TR)]
    two = [second_phase(i) for i in range(TR)]
    for i in range(TR):
        begin(one[i][:2])

    finish(panel_z_copies + diag_z_copies)
    partner = (2 * z + 1 - core, col)
    core_copies = [
        copy(diag_all.at[:, core], diag_all.at[:, core], sems(), partner),
        copy(panel_all.at[:, core], panel_all.at[:, core], sems(), partner),
    ]
    begin(core_copies)

    for i in range(TR):
        one[i][0].wait_recv()
        begin([one[i][2]])
        one[i][1].wait_recv()
        begin([one[i][3]])
    for i in range(TR):
        finish(one[i][2:])
        begin(two[i][:2])

    finish(core_copies)
    tile = diag_all[...].reshape(B, B)
    high, low_part = split(tile)
    pivot_high = dot(pivoting, high, NN)
    pivot_low = dot(pivoting, low_part, NN)
    scale = 1.0 / jnp.sum(jnp.where(wide_eye, pivot_high + pivot_low, 0.0), axis=0, keepdims=True)
    pivot_high, pivot_low = pivot_high.astype(BF16), pivot_low.astype(BF16)
    left = jnp.concatenate(
        [panel_all[a, b, :, 0].reshape(TC * K, 64) for a in range(4) for b in range(2)], axis=1
    )
    neg_v[...] = -jnp.concatenate(
        [panel_all[a, b, :, 1].reshape(TC * K, 64) for a in range(4) for b in range(2)], axis=1
    )
    lead = dot(left, pivoting, NT)
    kept = jnp.concatenate(
        [jnp.full((K, 1), pattern[j].astype(F32), F32) for j in range(TC)], axis=0
    )
    lead = lead * kept

    def through_pivot(a):
        return halves_dot(a, pivot_high, pivot_low, NT)

    def once(a):
        scaled = a * scale
        return 2.0 * scaled - through_pivot(scaled) * scale

    inner = once(lead)
    images = (2.0 * inner - once(through_pivot(inner))).astype(BF16)

    for i in range(TR):
        two[i][0].wait_recv()
        begin([two[i][2]])
        two[i][1].wait_recv()
        begin([two[i][3]])
    for i in range(TR):
        finish(two[i][2:])
        products[i] = dot(images, grid[i].reshape(B, B), NT).astype(BF16)

    for c in started:
        c.wait_send()
    pltpu.make_async_copy(near_all, near_all, near_sems[0]).wait()


def exchange(*operands):
    vmem = pl.BlockSpec(memory_space=pltpu.VMEM)
    smem = pl.BlockSpec(memory_space=pltpu.SMEM)
    dma = pltpu.SemaphoreType.DMA
    return pl.pallas_call(
        exchange_kernel,
        out_shape=(
            jax.ShapeDtypeStruct((TR, TC * K, B), BF16),
            jax.ShapeDtypeStruct((TC * K, B), BF16),
        ),
        in_specs=[vmem, vmem, vmem, smem, vmem, vmem, vmem, vmem, smem],
        out_specs=(vmem, vmem),
        scratch_shapes=[
            pltpu.VMEM((N_DEV, 16, 128), BF16),
            pltpu.VMEM((N_DEV, 16, 128), BF16),
            pltpu.VMEM((32, 128), BF16),
            pltpu.VMEM((8, 32, 128), BF16),
            pltpu.VMEM((16, 32, 128), BF16),
            pltpu.VMEM((4, 16, B), F32),
            pltpu.VMEM((4, 2, 64, B), F32),
            pltpu.VMEM((4, 2, TC, 2, K, 64), BF16),
            pltpu.VMEM((TR, 4, 4, RB, B), BF16),
            dma((48,)),
            dma((48,)),
            dma((TR, 2, 4)),
            dma((TR, 2, 4)),
        ],
        compiler_params=pltpu.CompilerParams(
            collective_id=0, has_side_effects=True, vmem_limit_bytes=56 << 20
        ),
    )(*operands)


def update_kernel(ranks, trail, products, neg_v, out):
    i = pl.program_id(0)
    half = pl.program_id(1)
    for j in range(2):
        rank = ranks[i, half * 2 + j]
        left = jnp.where(iota((K, B), 0) < rank, trail[0, j, 0], jnp.zeros((), BF16))
        rows = pl.ds(K * j, K)
        lhs = jnp.concatenate([left, products[0, rows]], axis=0)
        rhs = jnp.concatenate([trail[0, j, 1], neg_v[rows]], axis=0)
        out[0, j] = dot(lhs, rhs, TN).astype(BF16)


def update(ranks, trail, products, neg_v):
    return pl.pallas_call(
        update_kernel,
        grid=(TR, 2),
        out_shape=jax.ShapeDtypeStruct((TR, TC, B, B), BF16),
        in_specs=[
            pl.BlockSpec(memory_space=pltpu.SMEM),
            pl.BlockSpec((1, 2, 2, K, B), lambda i, h: (i, h, 0, 0, 0)),
            pl.BlockSpec((1, 2 * K, B), lambda i, h: (i, h, 0)),
            pl.BlockSpec((2 * K, B), lambda i, h: (h, 0)),
        ],
        out_specs=pl.BlockSpec((1, 2, B, B), lambda i, h: (i, h, 0, 0)),
        compiler_params=pltpu.CompilerParams(vmem_limit_bytes=32 << 20),
    )(ranks, trail, products, neg_v)


def per_device(
    diag_tile,
    pivot_order,
    panel_col,
    panel_row,
    trail_factors,
    tile_ranks,
    pattern,
    near_vals,
    near_dest,
    near_row,
    near_count,
):
    products, neg_v = exchange(
        near_vals,
        near_dest,
        near_row.reshape(1, NEAR),
        near_count,
        panel_col,
        diag_tile,
        pivot_order.reshape(1, B),
        panel_row,
        pattern,
    )
    return update(tile_ranks, trail_factors, products, neg_v)


def solution(mesh):
    placed = (
        P(("row", "col"), None),
        P(),
        P("row", "col", None),
        P("col", None, None, "row"),
        P("row", "col", None, None, None),
        P("row", "col"),
        P("col"),
        P(("row", "col"), None),
        P(("row", "col"), None),
        P(("row", "col")),
        P(("row", "col")),
    )
    return jax.shard_map(
        per_device,
        mesh=mesh,
        in_specs=placed,
        out_specs=P("row", "col", None, None),
        check_vma=False,
    )
```

```python
import jax
import jax.numpy as jnp
from jax import lax
from jax.experimental import pallas as pl
from jax.experimental.pallas import tpu as pltpu
from jax.sharding import PartitionSpec as P

B = 512
K = 64
TR = 8
TC = 4
NEAR = 256
CAP = 4
RB = 32
N_ROW = 8
N_COL = 16
N_DEV = 128
N_IN = 10
MESH = pl.DeviceIdType.MESH
F32 = jnp.float32
BF16 = jnp.bfloat16
NN = (((1,), (0,)), ((), ()))
NT = (((1,), (1,)), ((), ()))
TN = (((0,), (0,)), ((), ()))


def dot(a, b, dims):
    return lax.dot_general(a, b, dims, preferred_element_type=F32)


def iota(shape, dim):
    return lax.broadcasted_iota(jnp.int32, shape, dim)


def split(a):
    high = a.astype(BF16)
    return high, (a - high.astype(F32)).astype(BF16)


def halves_dot(a, b_high, b_low, dims):
    a_high, a_low = split(a)
    return dot(a_high, b_high, dims) + (dot(a_high, b_low, dims) + dot(a_low, b_high, dims))


def exchange_kernel(near_count, *refs):
    sources, (lefts, rights) = refs[:N_IN], refs[N_IN : N_IN + 2]
    held, local_sems = refs[N_IN + 2 : 2 * N_IN + 1], refs[2 * N_IN + 1]
    near_dest, near_row, near_vals, diag_tile, panel_row, pivot_order, pattern, panel_col, ranks = held
    (
    near_out,
    near_in,
    meta_own,
    meta_row,
    meta_all,
    diag_x,
    diag_all,
    panel_all,
    grid,
    one_send,
    one_recv,
    ring_send,
    ring_recv,
    ) = refs[2 * N_IN + 2 :]
    loads = [
        pltpu.make_async_copy(source, place, local_sems.at[k])
        for k, (source, place) in enumerate(zip(sources, held))
    ]
    trail = sources[-1]
    loads.append(pltpu.make_async_copy(trail.at[:, :, 0], lefts.at[:, :, pl.ds(0, K)], local_sems.at[N_IN]))
    loads.append(pltpu.make_async_copy(trail.at[:, :, 1], rights.at[:, :, pl.ds(0, K)], local_sems.at[N_IN + 1]))
    for load in loads:
        load.start()

    row = lax.axis_index("row")
    col = lax.axis_index("col")
    y, x = col // 4, lax.rem(col, 4)
    z, core = row // 2, lax.rem(row, 2)
    me = row * N_COL + col
    me_in = col * N_ROW + row

    def up(v):
        return lax.rem(v + 1, 4)

    def down(v):
        return lax.rem(v + 3, 4)

    barrier = pltpu.get_barrier_semaphore()

    def greet(step, carry):
        other = lax.rem(me + step, N_DEV)
        pl.semaphore_signal(
            barrier, inc=1, device_id=(other // N_COL, lax.rem(other, N_COL)), device_id_type=MESH
        )
        return carry

    lax.fori_loop(1, N_DEV, greet, 0)

    def copy(src, dst, sems, device):
        return pltpu.make_async_remote_copy(
            src_ref=src,
            dst_ref=dst,
            send_sem=sems[0],
            recv_sem=sems[1],
            device_id=device,
            device_id_type=MESH,
        )

    for load in loads[:3]:
        load.wait()

    dest_lane = near_dest[...]
    eye = iota((NEAR, NEAR), 0) == iota((NEAR, NEAR), 1)
    dest_col = jnp.sum(jnp.where(eye, dest_lane, 0), axis=1, keepdims=True)
    row_col = jnp.sum(jnp.where(eye, near_row[...], 0), axis=1, keepdims=True)
    earlier = (dest_col == dest_lane) & (iota((NEAR, NEAR), 1) < iota((NEAR, NEAR), 0))
    position = jnp.sum(jnp.where(earlier, 1, 0), axis=1, keepdims=True)
    live = iota((NEAR, 1), 0) < near_count[0]
    slot = jnp.where(live, dest_col * CAP + position, -1)
    placing = slot == iota((NEAR, N_DEV * CAP), 1)
    table = jnp.sum(jnp.where(placing, (row_col + 1).astype(F32), 0.0), axis=0, keepdims=True)
    placed = dot(jnp.where(placing, 1.0, 0.0).astype(BF16), near_vals[...], TN)
    low = iota((64, 8, 128), 1) < 4
    pieces = [placed[:, 128 * b : 128 * b + 128].reshape(64, 8, 128) for b in range(4)]
    turned = [pltpu.roll(p, 4, 1) for p in pieces]
    even = jnp.concatenate(
        [jnp.where(low, pieces[0], turned[1]), jnp.where(low, pieces[2], turned[3])], axis=1
    )
    odd = jnp.concatenate(
        [jnp.where(low, turned[0], pieces[1]), jnp.where(low, turned[2], pieces[3])], axis=1
    )
    both = jnp.concatenate([even[:, None], odd[:, None]], axis=1)
    near_out[...] = both.reshape(N_DEV, 16, 128).astype(BF16)

    meta = jnp.zeros((32, 128), F32)
    for m in range(4):
        meta = meta + jnp.where(
            iota((32, 128), 0) == 4 * row + m, table[:, 128 * m : 128 * m + 128], 0.0
        )
    meta_own[...] = meta.astype(BF16)

    for load in loads[3:9]:
        load.wait()

    own_rows = diag_tile[...]
    diag_x[x] = jnp.where(
        iota((16, B), 0) // 4 == x, jnp.concatenate([own_rows] * 4, axis=0), 0.0
    )
    panel_all[z, core] = panel_row[...]

    pl.semaphore_wait(barrier, N_DEV - 1)

    ones = iter(range(64))

    def sems():
        k = next(ones)
        return one_send.at[k], one_recv.at[k]

    def finish(copies):
        for c in copies:
            c.wait_recv()

    started = []

    def begin(copies):
        for c in copies:
            c.start()
        started.extend(copies)

    meta_row_copies = []
    for k in range(1, N_ROW):
        meta_row_copies.append(
            copy(meta_own, meta_row.at[k], sems(), (lax.rem(row + k, N_ROW), col))
        )
    begin(meta_row_copies)
    diag_x_copies = [
        copy(diag_x.at[x], diag_x.at[x], sems(), (row, 4 * y + lax.rem(x + k, 4))) for k in (1, 3, 2)
    ]
    begin(diag_x_copies)

    near_sems = sems()

    def send_near(step, carry):
        other = lax.rem(me + step, N_DEV)
        copy(
            near_out.at[other],
            near_in.at[me_in],
            near_sems,
            (other // N_COL, lax.rem(other, N_COL)),
        ).start()
        return carry

    lax.fori_loop(1, N_DEV, send_near, 0)
    near_in[me_in] = near_out[me]

    finish(meta_row_copies)
    total = meta_own[...].astype(F32)
    for k in range(1, N_ROW):
        total = total + meta_row[k].astype(F32)
    meta_all[col] = total.astype(BF16)
    meta_copies = [
        copy(meta_all.at[col], meta_all.at[col], sems(), (row, lax.rem(col + k, N_COL)))
        for k in range(1, N_COL)
    ]
    begin(meta_copies)

    finish(diag_x_copies)
    mine = diag_all.at[z, core, pl.ds(pl.multiple_of(16 * y, 16), 16)]
    mine[...] = (diag_x[0] + diag_x[1]) + (diag_x[2] + diag_x[3])
    diag_y_copies = [copy(mine, mine, sems(), (row, 4 * lax.rem(y + k, 4) + x)) for k in (1, 3, 2)]
    begin(diag_y_copies)

    finish(meta_copies)
    slots = N_DEV * CAP
    ids = iota((slots, 1), 0)
    wanted = (ids // CAP) * CAP + me // 32
    choose = jnp.where(iota((slots, slots), 1) == wanted, 1.0, 0.0).astype(BF16)
    named = dot(choose, meta_all[...].reshape(slots, 128), NN)
    lane = lax.rem(me, 32) * CAP + lax.rem(ids, CAP)
    target = jnp.sum(jnp.where(iota((slots, 128), 1) == lane, named, 0.0), axis=1, keepdims=True)
    landing = jnp.where(target.astype(jnp.int32) - 1 == iota((slots, 256), 1), 1.0, 0.0).astype(BF16)

    finish(diag_y_copies)
    near_all = near_in.at[pl.ds(0, N_DEV - 1)]
    pltpu.make_async_copy(near_all, near_all, near_sems[1]).wait()
    both = near_in[...].astype(F32).reshape(64, 2, 16, 128)
    even, odd = both[:, 0], both[:, 1]
    columns = []
    for b in range(0, 4, 2):
        first, second = even[:, 4 * b : 4 * b + 8], odd[:, 4 * b : 4 * b + 8]
        columns.append(jnp.where(low, first, pltpu.roll(second, 4, 1)).reshape(slots, 128))
        columns.append(jnp.where(low, pltpu.roll(first, 4, 1), second).reshape(slots, 128))
    arrived = jnp.concatenate(columns, axis=1).astype(BF16)
    additions = dot(landing, arrived, TN)
    corrected = (panel_col[...].astype(F32) + additions.reshape(TR, RB, B)).astype(BF16)
    for i in range(TR):
        grid[i, y, x] = corrected[i]

    def ring_copy(i, phase, k, part, device):
        return copy(part, part, (ring_send.at[i, phase, k], ring_recv.at[i, phase, k]), device)

    def first_phase(i):
        if i % 2 == 0:
            plus, minus = (row, 4 * y + up(x)), (row, 4 * y + down(x))
            before, after = grid.at[i, y, down(x)], grid.at[i, y, up(x)]
        else:
            plus, minus = (row, 4 * up(y) + x), (row, 4 * down(y) + x)
            before, after = grid.at[i, down(y), x], grid.at[i, up(y), x]
        own = grid.at[i, y, x]
        return (
            ring_copy(i, 0, 0, own, plus),
            ring_copy(i, 0, 1, own, minus),
            ring_copy(i, 0, 2, before.at[pl.ds(0, 16)], plus),
            ring_copy(i, 0, 3, after.at[pl.ds(16, 16)], minus),
        )

    def second_phase(i):
        if i % 2 == 0:
            plus, minus = (row, 4 * up(y) + x), (row, 4 * down(y) + x)
            own = grid.at[i, y]
            before, after = grid.at[i, down(y), pl.ds(0, 2)], grid.at[i, up(y), pl.ds(2, 2)]
        else:
            plus, minus = (row, 4 * y + up(x)), (row, 4 * y + down(x))
            own = grid.at[i, :, x]
            before, after = grid.at[i, pl.ds(0, 2), down(x)], grid.at[i, pl.ds(2, 2), up(x)]
        return (
            ring_copy(i, 1, 0, own, plus),
            ring_copy(i, 1, 1, own, minus),
            ring_copy(i, 1, 2, before, plus),
            ring_copy(i, 1, 3, after, minus),
        )

    one = [first_phase(i) for i in range(TR)]
    two = [second_phase(i) for i in range(TR)]
    for i in range(TR):
        begin(one[i][:2])
    diag_z_copies = [
        copy(
            diag_all.at[z, core],
            diag_all.at[z, core],
            sems(),
            (2 * lax.rem(z + k, 4) + core, col),
        )
        for k in (1, 3, 2)
    ]
    begin(diag_z_copies)

    panel_z_copies = [
        copy(
            panel_all.at[z, core],
            panel_all.at[z, core],
            sems(),
            (2 * lax.rem(z + k, 4) + core, col),
        )
        for k in (1, 3, 2)
    ]
    begin(panel_z_copies)


    for i in range(TR):
        one[i][0].wait_recv()
        begin([one[i][2]])
        one[i][1].wait_recv()
        begin([one[i][3]])
    for i in range(TR):
        finish(one[i][2:])
        begin(two[i][:2])

    for i in range(0, 4):
        two[i][0].wait_recv()
        begin([two[i][2]])
        two[i][1].wait_recv()
        begin([two[i][3]])
    finish(panel_z_copies + diag_z_copies)
    partner = (2 * z + 1 - core, col)
    core_copies = [
        copy(diag_all.at[:, core], diag_all.at[:, core], sems(), partner),
        copy(panel_all.at[:, core], panel_all.at[:, core], sems(), partner),
    ]
    begin(core_copies)

    wide_eye = iota((B, B), 0) == iota((B, B), 1)
    pivot_col = jnp.sum(jnp.where(wide_eye, pivot_order[...], 0), axis=1, keepdims=True)
    pivoting = jnp.where(pivot_col == iota((B, B), 1), 1.0, 0.0).astype(BF16)

    for i in range(4, 8):
        two[i][0].wait_recv()
        begin([two[i][2]])
        two[i][1].wait_recv()
        begin([two[i][3]])

    finish(core_copies)
    tile = diag_all[...].reshape(B, B)
    high, low_part = split(tile)
    pivot_high = dot(pivoting, high, NN)
    pivot_low = dot(pivoting, low_part, NN)
    scale = 1.0 / jnp.sum(jnp.where(wide_eye, pivot_high + pivot_low, 0.0), axis=0, keepdims=True)
    pivot_high, pivot_low = pivot_high.astype(BF16), pivot_low.astype(BF16)
    left = jnp.concatenate(
        [panel_all[a, b, :, 0].reshape(TC * K, 64) for a in range(4) for b in range(2)], axis=1
    )
    neg_v = -jnp.concatenate(
        [panel_all[a, b, :, 1].reshape(TC * K, 64) for a in range(4) for b in range(2)], axis=1
    )
    lead = dot(left, pivoting, NT)
    kept = jnp.concatenate(
        [jnp.broadcast_to(pattern[:, j : j + 1], (K, 1)) for j in range(TC)], axis=0
    )
    lead = lead * kept.astype(F32)

    def through_pivot(a):
        return halves_dot(a, pivot_high, pivot_low, NT)

    def once(a):
        scaled = a * scale
        return 2.0 * scaled - through_pivot(scaled) * scale

    inner = once(lead)
    images = (2.0 * inner - once(through_pivot(inner))).astype(BF16)

    for load in loads[9:]:
        load.wait()
    for i in range(TR):
        for j in range(TC):
            kept = iota((K, B), 0) < ranks[j : j + 1, i : i + 1]
            lefts[i, j, 0:K] = jnp.where(kept, lefts[i, j, 0:K], jnp.zeros((), BF16))
            rights[i, j, K : 2 * K] = neg_v[K * j : K * j + K]

    for i in range(TR):
        finish(two[i][2:])
        product = dot(images, grid[i].reshape(B, B), NT).astype(BF16)
        for j in range(TC):
            lefts[i, j, K : 2 * K] = product[K * j : K * j + K]

    for c in started:
        c.wait_send()
    pltpu.make_async_copy(near_all, near_all, near_sems[0]).wait()


def exchange(near_count, *operands):
    vmem = pl.BlockSpec(memory_space=pltpu.VMEM)
    hbm = pl.BlockSpec(memory_space=pltpu.HBM)
    dma = pltpu.SemaphoreType.DMA
    return pl.pallas_call(
        exchange_kernel,
        out_shape=(
            jax.ShapeDtypeStruct((TR, TC, 2 * K, B), BF16),
            jax.ShapeDtypeStruct((TR, TC, 2 * K, B), BF16),
        ),
        in_specs=[pl.BlockSpec(memory_space=pltpu.SMEM)] + [hbm] * N_IN,
        out_specs=(vmem, vmem),
        scratch_shapes=[
            *[pltpu.VMEM(a.shape, a.dtype) for a in operands[:-1]],
            dma((N_IN + 2,)),
            pltpu.VMEM((N_DEV, 16, 128), BF16),
            pltpu.VMEM((N_DEV, 16, 128), BF16),
            pltpu.VMEM((32, 128), BF16),
            pltpu.VMEM((8, 32, 128), BF16),
            pltpu.VMEM((16, 32, 128), BF16),
            pltpu.VMEM((4, 16, B), F32),
            pltpu.VMEM((4, 2, 64, B), F32),
            pltpu.VMEM((4, 2, TC, 2, K, 64), BF16),
            pltpu.VMEM((TR, 4, 4, RB, B), BF16),
            dma((48,)),
            dma((48,)),
            dma((TR, 2, 4)),
            dma((TR, 2, 4)),
        ],
        compiler_params=pltpu.CompilerParams(
            collective_id=0, has_side_effects=True, vmem_limit_bytes=28 << 20
        ),
    )(near_count, *[pltpu.with_memory_space_constraint(a, pltpu.HBM) for a in operands])


def update_kernel(lefts, rights, out, made, sems):
    copies = []
    for i in range(TR):
        for j in range(TC):
            made[i, j] = dot(lefts[i, j], rights[i, j], TN).astype(BF16)
            copies.append(pltpu.make_async_copy(made.at[i, j], out.at[i, j], sems.at[i, j]))
            copies[-1].start()
    for copy in copies:
        copy.wait()


def update(lefts, rights):
    vmem = pl.BlockSpec(memory_space=pltpu.VMEM)
    return pl.pallas_call(
        update_kernel,
        out_shape=jax.ShapeDtypeStruct((TR, TC, B, B), BF16),
        in_specs=[vmem, vmem],
        out_specs=pl.BlockSpec(memory_space=pltpu.HBM),
        scratch_shapes=[
            pltpu.VMEM((TR, TC, B, B), BF16),
            pltpu.SemaphoreType.DMA((TR, TC)),
        ],
        compiler_params=pltpu.CompilerParams(vmem_limit_bytes=30 << 20),
    )(lefts, rights)


def per_device(
    diag_tile,
    pivot_order,
    panel_col,
    panel_row,
    trail_factors,
    tile_ranks,
    pattern,
    near_vals,
    near_dest,
    near_row,
    near_count,
):
    lefts, rights = exchange(
        near_count,
        near_dest.reshape(1, NEAR),
        near_row.reshape(1, NEAR),
        near_vals,
        diag_tile,
        panel_row,
        pivot_order.reshape(1, B),
        pattern.reshape(1, TC),
        panel_col,
        tile_ranks.T,
        trail_factors,
    )
    return update(lefts, rights)


def solution(mesh):
    placed = (
        P(("row", "col"), None),
        P(),
        P("row", "col", None),
        P("col", None, None, "row"),
        P("row", "col", None, None, None),
        P("row", "col"),
        P("col"),
        P(("row", "col"), None),
        P(("row", "col"), None),
        P(("row", "col")),
        P(("row", "col")),
    )
    return jax.shard_map(
        per_device,
        mesh=mesh,
        in_specs=placed,
        out_specs=P("row", "col", None, None),
        check_vma=False,
    )
```

```python
import jax
import jax.numpy as jnp
from jax import lax
from jax.experimental import pallas as pl
from jax.experimental.pallas import tpu as pltpu
from jax.sharding import PartitionSpec as P

B = 512
K = 64
TR = 8
TC = 4
NEAR = 256
CAP = 4
RB = 32
N_ROW = 8
N_COL = 16
N_DEV = 128
N_IN = 10
MESH = pl.DeviceIdType.MESH
F32 = jnp.float32
BF16 = jnp.bfloat16
NN = (((1,), (0,)), ((), ()))
NT = (((1,), (1,)), ((), ()))
TN = (((0,), (0,)), ((), ()))


def dot(a, b, dims):
    return lax.dot_general(a, b, dims, preferred_element_type=F32)


def iota(shape, dim):
    return lax.broadcasted_iota(jnp.int32, shape, dim)


def split(a):
    high = a.astype(BF16)
    return high, (a - high.astype(F32)).astype(BF16)


def halves_dot(a, b_high, b_low, dims):
    a_high, a_low = split(a)
    return dot(a_high, b_high, dims) + (dot(a_high, b_low, dims) + dot(a_low, b_high, dims))


def exchange_kernel(near_count, *refs):
    sources, (lefts, rights) = refs[:N_IN], refs[N_IN : N_IN + 2]
    held, local_sems = refs[N_IN + 2 : 2 * N_IN + 1], refs[2 * N_IN + 1]
    near_dest, near_row, near_vals, diag_tile, panel_row, pivot_order, pattern, panel_col, ranks = held
    (
    near_out,
    near_in,
    meta_own,
    meta_row,
    meta_all,
    diag_x,
    diag_all,
    panel_all,
    grid,
    one_send,
    one_recv,
    ring_send,
    ring_recv,
    row_ready,
    ) = refs[2 * N_IN + 2 :]
    loads = [
        pltpu.make_async_copy(source, place, local_sems.at[k])
        for k, (source, place) in enumerate(zip(sources, held))
    ]
    trail = sources[-1]
    loads.append(pltpu.make_async_copy(trail.at[:, :, 0], lefts.at[:, :, pl.ds(0, K)], local_sems.at[N_IN]))
    loads.append(pltpu.make_async_copy(trail.at[:, :, 1], rights.at[:, :, pl.ds(0, K)], local_sems.at[N_IN + 1]))
    for load in loads:
        load.start()

    row = lax.axis_index("row")
    col = lax.axis_index("col")
    y, x = col // 4, lax.rem(col, 4)
    z, core = row // 2, lax.rem(row, 2)
    me = row * N_COL + col
    me_in = col * N_ROW + row

    def up(v):
        return lax.rem(v + 1, 4)

    def down(v):
        return lax.rem(v + 3, 4)

    barrier = pltpu.get_barrier_semaphore()

    row_peers = [(lax.rem(row + k, N_ROW), col) for k in range(1, N_ROW)]
    col_peers = [(row, lax.rem(col + k, N_COL)) for k in range(1, N_COL)]
    for peer in col_peers + row_peers:
        pl.semaphore_signal(barrier, inc=1, device_id=peer, device_id_type=MESH)
    pl.semaphore_wait(barrier, len(col_peers) + len(row_peers))
    for peer in col_peers:
        pl.semaphore_signal(row_ready, inc=1, device_id=peer, device_id_type=MESH)

    def copy(src, dst, sems, device):
        return pltpu.make_async_remote_copy(
            src_ref=src,
            dst_ref=dst,
            send_sem=sems[0],
            recv_sem=sems[1],
            device_id=device,
            device_id_type=MESH,
        )

    for load in loads[:3]:
        load.wait()

    dest_lane = near_dest[...]
    eye = iota((NEAR, NEAR), 0) == iota((NEAR, NEAR), 1)
    dest_col = jnp.sum(jnp.where(eye, dest_lane, 0), axis=1, keepdims=True)
    row_col = jnp.sum(jnp.where(eye, near_row[...], 0), axis=1, keepdims=True)
    earlier = (dest_col == dest_lane) & (iota((NEAR, NEAR), 1) < iota((NEAR, NEAR), 0))
    position = jnp.sum(jnp.where(earlier, 1, 0), axis=1, keepdims=True)
    live = iota((NEAR, 1), 0) < near_count[0]
    slot = jnp.where(live, dest_col * CAP + position, -1)
    placing = slot == iota((NEAR, N_DEV * CAP), 1)
    table = jnp.sum(jnp.where(placing, (row_col + 1).astype(F32), 0.0), axis=0, keepdims=True)
    placed = dot(jnp.where(placing, 1.0, 0.0).astype(BF16), near_vals[...], TN)
    low = iota((64, 8, 128), 1) < 4
    pieces = [placed[:, 128 * b : 128 * b + 128].reshape(64, 8, 128) for b in range(4)]
    turned = [pltpu.roll(p, 4, 1) for p in pieces]
    even = jnp.concatenate(
        [jnp.where(low, pieces[0], turned[1]), jnp.where(low, pieces[2], turned[3])], axis=1
    )
    odd = jnp.concatenate(
        [jnp.where(low, turned[0], pieces[1]), jnp.where(low, turned[2], pieces[3])], axis=1
    )
    both = jnp.concatenate([even[:, None], odd[:, None]], axis=1)
    near_out[...] = both.reshape(N_DEV, 16, 128).astype(BF16)

    meta = jnp.zeros((32, 128), F32)
    for m in range(4):
        meta = meta + jnp.where(
            iota((32, 128), 0) == 4 * row + m, table[:, 128 * m : 128 * m + 128], 0.0
        )
    meta_own[...] = meta.astype(BF16)

    for load in loads[3:9]:
        load.wait()

    own_rows = diag_tile[...]
    diag_x[x] = own_rows
    panel_all[z, core] = panel_row[...]


    ones = iter(range(64))

    def sems():
        k = next(ones)
        return one_send.at[k], one_recv.at[k]

    def finish(copies):
        for c in copies:
            c.wait_recv()

    started = []

    def begin(copies):
        for c in copies:
            c.start()
        started.extend(copies)

    meta_row_copies = []
    for k in range(1, N_ROW):
        meta_row_copies.append(
            copy(meta_own, meta_row.at[k], sems(), (lax.rem(row + k, N_ROW), col))
        )
    begin(meta_row_copies)
    diag_x_copies = [
        copy(diag_x.at[x], diag_x.at[x], sems(), (row, 4 * y + lax.rem(x + k, 4))) for k in (1, 3, 2)
    ]
    begin(diag_x_copies)

    near_sems = sems()

    def send_near(step, carry):
        other = lax.rem(me + step, N_DEV)
        copy(
            near_out.at[other],
            near_in.at[me_in],
            near_sems,
            (other // N_COL, lax.rem(other, N_COL)),
        ).start()
        return carry

    pl.semaphore_wait(row_ready, len(col_peers))
    lax.fori_loop(1, 65, send_near, 0)

    finish(meta_row_copies)
    total = meta_own[...].astype(F32)
    for k in range(1, N_ROW):
        total = total + meta_row[k].astype(F32)
    meta_all[col] = total.astype(BF16)
    meta_copies = [
        copy(meta_all.at[col], meta_all.at[col], sems(), (row, lax.rem(col + k, N_COL)))
        for k in range(1, N_COL)
    ]
    begin(meta_copies)
    lax.fori_loop(65, N_DEV, send_near, 0)
    near_in[me_in] = near_out[me]

    finish(meta_copies)
    slots = N_DEV * CAP
    ids = iota((slots, 1), 0)
    wanted = (ids // CAP) * CAP + me // 32
    choose = jnp.where(iota((slots, slots), 1) == wanted, 1.0, 0.0).astype(BF16)
    named = dot(choose, meta_all[...].reshape(slots, 128), NN)
    lane = lax.rem(me, 32) * CAP + lax.rem(ids, CAP)
    target = jnp.sum(jnp.where(iota((slots, 128), 1) == lane, named, 0.0), axis=1, keepdims=True)
    landing = jnp.where(target.astype(jnp.int32) - 1 == iota((slots, 256), 1), 1.0, 0.0).astype(BF16)

    near_all = near_in.at[pl.ds(0, N_DEV - 1)]
    pltpu.make_async_copy(near_all, near_all, near_sems[1]).wait()
    both = near_in[...].astype(F32).reshape(64, 2, 16, 128)
    even, odd = both[:, 0], both[:, 1]
    columns = []
    for b in range(0, 4, 2):
        first, second = even[:, 4 * b : 4 * b + 8], odd[:, 4 * b : 4 * b + 8]
        columns.append(jnp.where(low, first, pltpu.roll(second, 4, 1)).reshape(slots, 128))
        columns.append(jnp.where(low, pltpu.roll(first, 4, 1), second).reshape(slots, 128))
    arrived = jnp.concatenate(columns, axis=1).astype(BF16)
    additions = dot(landing, arrived, TN)
    corrected = (panel_col[...].astype(F32) + additions.reshape(TR, RB, B)).astype(BF16)
    for i in range(TR):
        grid[i, y, x] = corrected[i]

    def ring_copy(i, phase, k, part, device):
        return copy(part, part, (ring_send.at[i, phase, k], ring_recv.at[i, phase, k]), device)

    def first_phase(i):
        if i % 2 == 0:
            plus, minus = (row, 4 * y + up(x)), (row, 4 * y + down(x))
            before, after = grid.at[i, y, down(x)], grid.at[i, y, up(x)]
        else:
            plus, minus = (row, 4 * up(y) + x), (row, 4 * down(y) + x)
            before, after = grid.at[i, down(y), x], grid.at[i, up(y), x]
        own = grid.at[i, y, x]
        return (
            ring_copy(i, 0, 0, own, plus),
            ring_copy(i, 0, 1, own, minus),
            ring_copy(i, 0, 2, before.at[pl.ds(0, 16)], plus),
            ring_copy(i, 0, 3, after.at[pl.ds(16, 16)], minus),
        )

    def second_phase(i):
        if i % 2 == 0:
            plus, minus = (row, 4 * up(y) + x), (row, 4 * down(y) + x)
            own = grid.at[i, y]
            before, after = grid.at[i, down(y), pl.ds(0, 2)], grid.at[i, up(y), pl.ds(2, 2)]
        else:
            plus, minus = (row, 4 * y + up(x)), (row, 4 * y + down(x))
            own = grid.at[i, :, x]
            before, after = grid.at[i, pl.ds(0, 2), down(x)], grid.at[i, pl.ds(2, 2), up(x)]
        return (
            ring_copy(i, 1, 0, own, plus),
            ring_copy(i, 1, 1, own, minus),
            ring_copy(i, 1, 2, before, plus),
            ring_copy(i, 1, 3, after, minus),
        )

    one = [first_phase(i) for i in range(TR)]
    two = [second_phase(i) for i in range(TR)]
    for i in range(TR):
        begin(one[i][:2])
    finish(diag_x_copies)
    mine = diag_all.at[z, core, pl.ds(pl.multiple_of(16 * y, 16), 16)]
    mine[...] = jnp.concatenate([diag_x[k] for k in range(4)], axis=0)
    diag_y_copies = [copy(mine, mine, sems(), (row, 4 * lax.rem(y + k, 4) + x)) for k in (1, 3, 2)]
    begin(diag_y_copies)

    panel_z_copies = [
        copy(
            panel_all.at[z, core],
            panel_all.at[z, core],
            sems(),
            (2 * lax.rem(z + k, 4) + core, col),
        )
        for k in (1, 3, 2)
    ]
    begin(panel_z_copies)


    for i in range(TR):
        one[i][0].wait_recv()
        begin([one[i][2]])
        one[i][1].wait_recv()
        begin([one[i][3]])
    for i in range(TR):
        finish(one[i][2:])
        begin(two[i][:2])

    finish(diag_y_copies)
    diag_z_copies = [
        copy(
            diag_all.at[z, core],
            diag_all.at[z, core],
            sems(),
            (2 * lax.rem(z + k, 4) + core, col),
        )
        for k in (1, 3, 2)
    ]
    begin(diag_z_copies)


    for i in range(0, 4):
        two[i][0].wait_recv()
        begin([two[i][2]])
        two[i][1].wait_recv()
        begin([two[i][3]])
    finish(panel_z_copies + diag_z_copies)
    partner = (2 * z + 1 - core, col)
    core_copies = [
        copy(diag_all.at[:, core], diag_all.at[:, core], sems(), partner),
        copy(panel_all.at[:, core], panel_all.at[:, core], sems(), partner),
    ]
    begin(core_copies)

    wide_eye = iota((B, B), 0) == iota((B, B), 1)
    pivot_col = jnp.sum(jnp.where(wide_eye, pivot_order[...], 0), axis=1, keepdims=True)
    pivoting = jnp.where(pivot_col == iota((B, B), 1), 1.0, 0.0).astype(BF16)

    for i in range(4, 8):
        two[i][0].wait_recv()
        begin([two[i][2]])
        two[i][1].wait_recv()
        begin([two[i][3]])

    finish(core_copies)
    tile = diag_all[...].reshape(B, B)
    high, low_part = split(tile)
    pivot_high = dot(pivoting, high, NN)
    pivot_low = dot(pivoting, low_part, NN)
    scale = 1.0 / jnp.sum(jnp.where(wide_eye, pivot_high + pivot_low, 0.0), axis=0, keepdims=True)
    pivot_high, pivot_low = pivot_high.astype(BF16), pivot_low.astype(BF16)
    left = jnp.concatenate(
        [panel_all[a, b, :, 0].reshape(TC * K, 64) for a in range(4) for b in range(2)], axis=1
    )
    neg_v = -jnp.concatenate(
        [panel_all[a, b, :, 1].reshape(TC * K, 64) for a in range(4) for b in range(2)], axis=1
    )
    lead = dot(left, pivoting, NT)
    kept = jnp.concatenate(
        [jnp.broadcast_to(pattern[:, j : j + 1], (K, 1)) for j in range(TC)], axis=0
    )
    lead = lead * kept.astype(F32)

    def through_pivot(a):
        return halves_dot(a, pivot_high, pivot_low, NT)

    def once(a):
        scaled = a * scale
        return 2.0 * scaled - through_pivot(scaled) * scale

    inner = once(lead)
    images = (2.0 * inner - once(through_pivot(inner))).astype(BF16)

    for load in loads[9:]:
        load.wait()
    for i in range(TR):
        for j in range(TC):
            kept = iota((K, B), 0) < ranks[j : j + 1, i : i + 1]
            lefts[i, j, 0:K] = jnp.where(kept, lefts[i, j, 0:K], jnp.zeros((), BF16))
            rights[i, j, K : 2 * K] = neg_v[K * j : K * j + K]

    for i in range(TR):
        finish(two[i][2:])
        product = dot(images, grid[i].reshape(B, B), NT).astype(BF16)
        for j in range(TC):
            lefts[i, j, K : 2 * K] = product[K * j : K * j + K]

    for c in started:
        c.wait_send()
    pltpu.make_async_copy(near_all, near_all, near_sems[0]).wait()


def exchange(near_count, *operands):
    vmem = pl.BlockSpec(memory_space=pltpu.VMEM)
    hbm = pl.BlockSpec(memory_space=pltpu.HBM)
    dma = pltpu.SemaphoreType.DMA
    return pl.pallas_call(
        exchange_kernel,
        out_shape=(
            jax.ShapeDtypeStruct((TR, TC, 2 * K, B), BF16),
            jax.ShapeDtypeStruct((TR, TC, 2 * K, B), BF16),
        ),
        in_specs=[pl.BlockSpec(memory_space=pltpu.SMEM)] + [hbm] * N_IN,
        out_specs=(vmem, vmem),
        scratch_shapes=[
            *[pltpu.VMEM(a.shape, a.dtype) for a in operands[:-1]],
            dma((N_IN + 2,)),
            pltpu.VMEM((N_DEV, 16, 128), BF16),
            pltpu.VMEM((N_DEV, 16, 128), BF16),
            pltpu.VMEM((32, 128), BF16),
            pltpu.VMEM((8, 32, 128), BF16),
            pltpu.VMEM((16, 32, 128), BF16),
            pltpu.VMEM((4, 4, B), F32),
            pltpu.VMEM((4, 2, 64, B), F32),
            pltpu.VMEM((4, 2, TC, 2, K, 64), BF16),
            pltpu.VMEM((TR, 4, 4, RB, B), BF16),
            dma((48,)),
            dma((48,)),
            dma((TR, 2, 4)),
            dma((TR, 2, 4)),
            pltpu.SemaphoreType.REGULAR,
        ],
        compiler_params=pltpu.CompilerParams(
            collective_id=0, has_side_effects=True, vmem_limit_bytes=28 << 20
        ),
    )(near_count, *[pltpu.with_memory_space_constraint(a, pltpu.HBM) for a in operands])


def update_kernel(lefts, rights, out, made, sems):
    copies = []
    for i in range(TR):
        for j in range(TC):
            made[i, j] = dot(lefts[i, j], rights[i, j], TN).astype(BF16)
            copies.append(pltpu.make_async_copy(made.at[i, j], out.at[i, j], sems.at[i, j]))
            copies[-1].start()
    for copy in copies:
        copy.wait()


def update(lefts, rights):
    vmem = pl.BlockSpec(memory_space=pltpu.VMEM)
    return pl.pallas_call(
        update_kernel,
        out_shape=jax.ShapeDtypeStruct((TR, TC, B, B), BF16),
        in_specs=[vmem, vmem],
        out_specs=pl.BlockSpec(memory_space=pltpu.HBM),
        scratch_shapes=[
            pltpu.VMEM((TR, TC, B, B), BF16),
            pltpu.SemaphoreType.DMA((TR, TC)),
        ],
        compiler_params=pltpu.CompilerParams(vmem_limit_bytes=30 << 20),
    )(lefts, rights)


def per_device(
    diag_tile,
    pivot_order,
    panel_col,
    panel_row,
    trail_factors,
    tile_ranks,
    pattern,
    near_vals,
    near_dest,
    near_row,
    near_count,
):
    lefts, rights = exchange(
        near_count,
        near_dest.reshape(1, NEAR),
        near_row.reshape(1, NEAR),
        near_vals,
        diag_tile,
        panel_row,
        pivot_order.reshape(1, B),
        pattern.reshape(1, TC),
        panel_col,
        tile_ranks.T,
        trail_factors,
    )
    return update(lefts, rights)


def solution(mesh):
    placed = (
        P(("row", "col"), None),
        P(),
        P("row", "col", None),
        P("col", None, None, "row"),
        P("row", "col", None, None, None),
        P("row", "col"),
        P("col"),
        P(("row", "col"), None),
        P(("row", "col"), None),
        P(("row", "col")),
        P(("row", "col")),
    )
    return jax.shard_map(
        per_device,
        mesh=mesh,
        in_specs=placed,
        out_specs=P("row", "col", None, None),
        check_vma=False,
    )
```

```python
import jax
import jax.numpy as jnp
from jax import lax
from jax.experimental import pallas as pl
from jax.experimental.pallas import tpu as pltpu
from jax.sharding import PartitionSpec as P

B = 512
K = 64
TR = 8
TC = 4
NEAR = 256
CAP = 4
RB = 32
N_ROW = 8
N_COL = 16
N_DEV = 128
N_IN = 10
MESH = pl.DeviceIdType.MESH
F32 = jnp.float32
BF16 = jnp.bfloat16
NN = (((1,), (0,)), ((), ()))
NT = (((1,), (1,)), ((), ()))
TN = (((0,), (0,)), ((), ()))


def dot(a, b, dims):
    return lax.dot_general(a, b, dims, preferred_element_type=F32)


def iota(shape, dim):
    return lax.broadcasted_iota(jnp.int32, shape, dim)


def split(a):
    high = a.astype(BF16)
    return high, (a - high.astype(F32)).astype(BF16)


def halves_dot(a, b_high, b_low, dims):
    a_high, a_low = split(a)
    return dot(a_high, b_high, dims) + (dot(a_high, b_low, dims) + dot(a_low, b_high, dims))


def exchange_kernel(near_count, *refs):
    sources, (lefts, rights) = refs[:N_IN], refs[N_IN : N_IN + 2]
    held, local_sems = refs[N_IN + 2 : 2 * N_IN + 1], refs[2 * N_IN + 1]
    near_dest, near_row, near_vals, diag_tile, panel_row, pivot_order, pattern, panel_col, ranks = held
    (
    near_out,
    near_in,
    meta_own,
    meta_row,
    meta_all,
    diag_x,
    diag_all,
    panel_all,
    grid,
    one_send,
    one_recv,
    ring_send,
    ring_recv,
    row_ready,
    ) = refs[2 * N_IN + 2 :]
    loads = [
        pltpu.make_async_copy(source, place, local_sems.at[k])
        for k, (source, place) in enumerate(zip(sources, held))
    ]
    trail = sources[-1]
    loads.append(pltpu.make_async_copy(trail.at[:, :, 0], lefts.at[:, :, pl.ds(0, K)], local_sems.at[N_IN]))
    loads.append(pltpu.make_async_copy(trail.at[:, :, 1], rights.at[:, :, pl.ds(0, K)], local_sems.at[N_IN + 1]))
    for load in loads:
        load.start()

    row = lax.axis_index("row")
    col = lax.axis_index("col")
    y, x = col // 4, lax.rem(col, 4)
    z, core = row // 2, lax.rem(row, 2)
    me = row * N_COL + col
    me_in = col * N_ROW + row

    def up(v):
        return lax.rem(v + 1, 4)

    def down(v):
        return lax.rem(v + 3, 4)

    barrier = pltpu.get_barrier_semaphore()

    row_peers = [(lax.rem(row + k, N_ROW), col) for k in range(1, N_ROW)]
    col_peers = [(row, lax.rem(col + k, N_COL)) for k in range(1, N_COL)]
    for peer in col_peers + row_peers:
        pl.semaphore_signal(barrier, inc=1, device_id=peer, device_id_type=MESH)
    pl.semaphore_wait(barrier, len(col_peers) + len(row_peers))
    for peer in row_peers:
        pl.semaphore_signal(row_ready, inc=1, device_id=peer, device_id_type=MESH)

    def copy(src, dst, sems, device):
        return pltpu.make_async_remote_copy(
            src_ref=src,
            dst_ref=dst,
            send_sem=sems[0],
            recv_sem=sems[1],
            device_id=device,
            device_id_type=MESH,
        )

    for load in loads[:3]:
        load.wait()

    dest_lane = near_dest[...]
    eye = iota((NEAR, NEAR), 0) == iota((NEAR, NEAR), 1)
    dest_col = jnp.sum(jnp.where(eye, dest_lane, 0), axis=1, keepdims=True)
    row_col = jnp.sum(jnp.where(eye, near_row[...], 0), axis=1, keepdims=True)
    earlier = (dest_col == dest_lane) & (iota((NEAR, NEAR), 1) < iota((NEAR, NEAR), 0))
    position = jnp.sum(jnp.where(earlier, 1, 0), axis=1, keepdims=True)
    live = iota((NEAR, 1), 0) < near_count[0]
    slot = jnp.where(live, dest_col * CAP + position, -1)
    placing = slot == iota((NEAR, N_DEV * CAP), 1)
    table = jnp.sum(jnp.where(placing, (row_col + 1).astype(F32), 0.0), axis=0, keepdims=True)
    placed = dot(jnp.where(placing, 1.0, 0.0).astype(BF16), near_vals[...], TN)
    low = iota((64, 8, 128), 1) < 4
    pieces = [placed[:, 128 * b : 128 * b + 128].reshape(64, 8, 128) for b in range(4)]
    turned = [pltpu.roll(p, 4, 1) for p in pieces]
    even = jnp.concatenate(
        [jnp.where(low, pieces[0], turned[1]), jnp.where(low, pieces[2], turned[3])], axis=1
    )
    odd = jnp.concatenate(
        [jnp.where(low, turned[0], pieces[1]), jnp.where(low, turned[2], pieces[3])], axis=1
    )
    both = jnp.concatenate([even[:, None], odd[:, None]], axis=1)
    near_out[...] = both.reshape(N_DEV, 16, 128).astype(BF16)

    meta = jnp.zeros((32, 128), F32)
    for m in range(4):
        meta = meta + jnp.where(
            iota((32, 128), 0) == 4 * row + m, table[:, 128 * m : 128 * m + 128], 0.0
        )
    meta_own[...] = meta.astype(BF16)

    for load in loads[3:9]:
        load.wait()

    own_rows = diag_tile[...]
    diag_x[x] = own_rows
    panel_all[z, core] = panel_row[...]


    ones = iter(range(64))

    def sems():
        k = next(ones)
        return one_send.at[k], one_recv.at[k]

    def finish(copies):
        for c in copies:
            c.wait_recv()

    started = []

    def begin(copies):
        for c in copies:
            c.start()
        started.extend(copies)

    meta_row_copies = []
    for k in range(1, N_ROW):
        meta_row_copies.append(
            copy(meta_own, meta_row.at[k], sems(), (lax.rem(row + k, N_ROW), col))
        )
    begin(meta_row_copies)
    diag_x_copies = [
        copy(diag_x.at[x], diag_x.at[x], sems(), (row, 4 * y + lax.rem(x + k, 4))) for k in (1, 3, 2)
    ]
    begin(diag_x_copies)

    near_sems = sems()

    def send_near(target_row, target_col):
        other = target_row * N_COL + target_col
        copy(near_out.at[other], near_in.at[me_in], near_sems, (target_row, target_col)).start()

    offsets = [
        (dz, dcore, dy, dx)
        for dz in range(4)
        for dcore in range(2)
        for dy in range(4)
        for dx in range(4)
        if (dz, dcore) != (0, 0) or (dy, dx) != (0, 0)
    ]
    hops = [0, 1, 2, 1]
    offsets.sort(key=lambda o: (-hops[o[0]] - hops[o[2]] - hops[o[3]], (7 * o[0] + 5 * o[2] + 3 * o[3] + o[1]) % 8))

    def send_far(some):
        for dz, dcore, dy, dx in some:
            other_core = lax.rem(core + dcore, 2)
            send_near(
                2 * lax.rem(z + dz, 4) + other_core, 4 * lax.rem(y + dy, 4) + lax.rem(x + dx, 4)
            )

    pl.semaphore_wait(row_ready, len(row_peers))
    send_far(offsets[:80])

    finish(meta_row_copies)
    total = meta_own[...].astype(F32)
    for k in range(1, N_ROW):
        total = total + meta_row[k].astype(F32)
    meta_all[col] = total.astype(BF16)
    meta_copies = [
        copy(meta_all.at[col], meta_all.at[col], sems(), (row, lax.rem(col + k, N_COL)))
        for k in range(1, N_COL)
    ]
    begin(meta_copies)
    send_far(offsets[80:])
    near_in[me_in] = near_out[me]

    finish(diag_x_copies)
    mine = diag_all.at[z, core, pl.ds(pl.multiple_of(16 * y, 16), 16)]
    mine[...] = jnp.concatenate([diag_x[k] for k in range(4)], axis=0)
    diag_y_copies = [copy(mine, mine, sems(), (row, 4 * lax.rem(y + k, 4) + x)) for k in (1, 3, 2)]
    begin(diag_y_copies)


    finish(meta_copies)
    slots = N_DEV * CAP
    ids = iota((slots, 1), 0)
    wanted = (ids // CAP) * CAP + me // 32
    choose = jnp.where(iota((slots, slots), 1) == wanted, 1.0, 0.0).astype(BF16)
    named = dot(choose, meta_all[...].reshape(slots, 128), NN)
    lane = lax.rem(me, 32) * CAP + lax.rem(ids, CAP)
    target = jnp.sum(jnp.where(iota((slots, 128), 1) == lane, named, 0.0), axis=1, keepdims=True)
    landing = jnp.where(target.astype(jnp.int32) - 1 == iota((slots, 256), 1), 1.0, 0.0).astype(BF16)

    near_all = near_in.at[pl.ds(0, N_DEV - 1)]
    pltpu.make_async_copy(near_all, near_all, near_sems[1]).wait()
    both = near_in[...].astype(F32).reshape(64, 2, 16, 128)
    even, odd = both[:, 0], both[:, 1]
    columns = []
    for b in range(0, 4, 2):
        first, second = even[:, 4 * b : 4 * b + 8], odd[:, 4 * b : 4 * b + 8]
        columns.append(jnp.where(low, first, pltpu.roll(second, 4, 1)).reshape(slots, 128))
        columns.append(jnp.where(low, pltpu.roll(first, 4, 1), second).reshape(slots, 128))
    arrived = jnp.concatenate(columns, axis=1).astype(BF16)
    additions = dot(landing, arrived, TN)
    corrected = (panel_col[...].astype(F32) + additions.reshape(TR, RB, B)).astype(BF16)
    for i in range(TR):
        grid[i, y, x] = corrected[i]

    def ring_copy(i, phase, k, part, device):
        return copy(part, part, (ring_send.at[i, phase, k], ring_recv.at[i, phase, k]), device)

    def first_phase(i):
        if i % 2 == 0:
            plus, minus = (row, 4 * y + up(x)), (row, 4 * y + down(x))
            before, after = grid.at[i, y, down(x)], grid.at[i, y, up(x)]
        else:
            plus, minus = (row, 4 * up(y) + x), (row, 4 * down(y) + x)
            before, after = grid.at[i, down(y), x], grid.at[i, up(y), x]
        own = grid.at[i, y, x]
        return (
            ring_copy(i, 0, 0, own, plus),
            ring_copy(i, 0, 1, own, minus),
            ring_copy(i, 0, 2, before.at[pl.ds(0, 16)], plus),
            ring_copy(i, 0, 3, after.at[pl.ds(16, 16)], minus),
        )

    def second_phase(i):
        if i % 2 == 0:
            plus, minus = (row, 4 * up(y) + x), (row, 4 * down(y) + x)
            own = grid.at[i, y]
            before, after = grid.at[i, down(y), pl.ds(0, 2)], grid.at[i, up(y), pl.ds(2, 2)]
        else:
            plus, minus = (row, 4 * y + up(x)), (row, 4 * y + down(x))
            own = grid.at[i, :, x]
            before, after = grid.at[i, pl.ds(0, 2), down(x)], grid.at[i, pl.ds(2, 2), up(x)]
        return (
            ring_copy(i, 1, 0, own, plus),
            ring_copy(i, 1, 1, own, minus),
            ring_copy(i, 1, 2, before, plus),
            ring_copy(i, 1, 3, after, minus),
        )

    one = [first_phase(i) for i in range(TR)]
    two = [second_phase(i) for i in range(TR)]
    for i in range(TR):
        begin(one[i][:2])
    panel_z_copies = [
        copy(
            panel_all.at[z, core],
            panel_all.at[z, core],
            sems(),
            (2 * lax.rem(z + k, 4) + core, col),
        )
        for k in (1, 3, 2)
    ]
    begin(panel_z_copies)


    for i in range(TR):
        one[i][0].wait_recv()
        begin([one[i][2]])
        one[i][1].wait_recv()
        begin([one[i][3]])
    finish(diag_y_copies)
    diag_z_copies = [
        copy(
            diag_all.at[z, core],
            diag_all.at[z, core],
            sems(),
            (2 * lax.rem(z + k, 4) + core, col),
        )
        for k in (1, 3, 2)
    ]
    begin(diag_z_copies)


    for i in range(TR):
        finish(one[i][2:])
        begin(two[i][:2])

    for i in range(0, 4):
        two[i][0].wait_recv()
        begin([two[i][2]])
        two[i][1].wait_recv()
        begin([two[i][3]])
    finish(panel_z_copies + diag_z_copies)
    partner = (2 * z + 1 - core, col)
    core_copies = [
        copy(diag_all.at[:, core], diag_all.at[:, core], sems(), partner),
        copy(panel_all.at[:, core], panel_all.at[:, core], sems(), partner),
    ]
    begin(core_copies)

    wide_eye = iota((B, B), 0) == iota((B, B), 1)
    pivot_col = jnp.sum(jnp.where(wide_eye, pivot_order[...], 0), axis=1, keepdims=True)
    pivoting = jnp.where(pivot_col == iota((B, B), 1), 1.0, 0.0).astype(BF16)

    for i in range(4, 6):
        two[i][0].wait_recv()
        begin([two[i][2]])
        two[i][1].wait_recv()
        begin([two[i][3]])
    finish(core_copies)
    tile = diag_all[...].reshape(B, B)
    high, low_part = split(tile)
    pivot_high = dot(pivoting, high, NN)
    pivot_low = dot(pivoting, low_part, NN)
    scale = 1.0 / jnp.sum(jnp.where(wide_eye, pivot_high + pivot_low, 0.0), axis=0, keepdims=True)
    pivot_high, pivot_low = pivot_high.astype(BF16), pivot_low.astype(BF16)
    left = jnp.concatenate(
        [panel_all[a, b, :, 0].reshape(TC * K, 64) for a in range(4) for b in range(2)], axis=1
    )
    neg_v = -jnp.concatenate(
        [panel_all[a, b, :, 1].reshape(TC * K, 64) for a in range(4) for b in range(2)], axis=1
    )
    lead = dot(left, pivoting, NT)
    kept = jnp.concatenate(
        [jnp.broadcast_to(pattern[:, j : j + 1], (K, 1)) for j in range(TC)], axis=0
    )
    lead = lead * kept.astype(F32)

    def through_pivot(a):
        return halves_dot(a, pivot_high, pivot_low, NT)

    def once(a):
        scaled = a * scale
        return 2.0 * scaled - through_pivot(scaled) * scale

    inner = once(lead)
    images = (2.0 * inner - once(through_pivot(inner))).astype(BF16)

    for i in range(6, 8):
        two[i][0].wait_recv()
        begin([two[i][2]])
        two[i][1].wait_recv()
        begin([two[i][3]])

    for load in loads[9:]:
        load.wait()
    for i in range(TR):
        for j in range(TC):
            kept = iota((K, B), 0) < ranks[j : j + 1, i : i + 1]
            lefts[i, j, 0:K] = jnp.where(kept, lefts[i, j, 0:K], jnp.zeros((), BF16))
            rights[i, j, K : 2 * K] = neg_v[K * j : K * j + K]

    for i in range(TR):
        finish(two[i][2:])
        product = dot(images, grid[i].reshape(B, B), NT).astype(BF16)
        for j in range(TC):
            lefts[i, j, K : 2 * K] = product[K * j : K * j + K]

    for c in started:
        c.wait_send()
    pltpu.make_async_copy(near_all, near_all, near_sems[0]).wait()


def exchange(near_count, *operands):
    vmem = pl.BlockSpec(memory_space=pltpu.VMEM)
    hbm = pl.BlockSpec(memory_space=pltpu.HBM)
    dma = pltpu.SemaphoreType.DMA
    return pl.pallas_call(
        exchange_kernel,
        out_shape=(
            jax.ShapeDtypeStruct((TR, TC, 2 * K, B), BF16),
            jax.ShapeDtypeStruct((TR, TC, 2 * K, B), BF16),
        ),
        in_specs=[pl.BlockSpec(memory_space=pltpu.SMEM)] + [hbm] * N_IN,
        out_specs=(vmem, vmem),
        scratch_shapes=[
            *[pltpu.VMEM(a.shape, a.dtype) for a in operands[:-1]],
            dma((N_IN + 2,)),
            pltpu.VMEM((N_DEV, 16, 128), BF16),
            pltpu.VMEM((N_DEV, 16, 128), BF16),
            pltpu.VMEM((32, 128), BF16),
            pltpu.VMEM((8, 32, 128), BF16),
            pltpu.VMEM((16, 32, 128), BF16),
            pltpu.VMEM((4, 4, B), F32),
            pltpu.VMEM((4, 2, 64, B), F32),
            pltpu.VMEM((4, 2, TC, 2, K, 64), BF16),
            pltpu.VMEM((TR, 4, 4, RB, B), BF16),
            dma((48,)),
            dma((48,)),
            dma((TR, 2, 4)),
            dma((TR, 2, 4)),
            pltpu.SemaphoreType.REGULAR,
        ],
        compiler_params=pltpu.CompilerParams(
            collective_id=0, has_side_effects=True, vmem_limit_bytes=28 << 20
        ),
    )(near_count, *[pltpu.with_memory_space_constraint(a, pltpu.HBM) for a in operands])


def update_kernel(lefts, rights, out, made, sems):
    copies = []
    for i in range(TR):
        for j in range(TC):
            made[i, j] = dot(lefts[i, j], rights[i, j], TN).astype(BF16)
            copies.append(pltpu.make_async_copy(made.at[i, j], out.at[i, j], sems.at[i, j]))
            copies[-1].start()
    for copy in copies:
        copy.wait()


def update(lefts, rights):
    vmem = pl.BlockSpec(memory_space=pltpu.VMEM)
    return pl.pallas_call(
        update_kernel,
        out_shape=jax.ShapeDtypeStruct((TR, TC, B, B), BF16),
        in_specs=[vmem, vmem],
        out_specs=pl.BlockSpec(memory_space=pltpu.HBM),
        scratch_shapes=[
            pltpu.VMEM((TR, TC, B, B), BF16),
            pltpu.SemaphoreType.DMA((TR, TC)),
        ],
        compiler_params=pltpu.CompilerParams(vmem_limit_bytes=30 << 20),
    )(lefts, rights)


def per_device(
    diag_tile,
    pivot_order,
    panel_col,
    panel_row,
    trail_factors,
    tile_ranks,
    pattern,
    near_vals,
    near_dest,
    near_row,
    near_count,
):
    lefts, rights = exchange(
        near_count,
        near_dest.reshape(1, NEAR),
        near_row.reshape(1, NEAR),
        near_vals,
        diag_tile,
        panel_row,
        pivot_order.reshape(1, B),
        pattern.reshape(1, TC),
        panel_col,
        tile_ranks.T,
        trail_factors,
    )
    return update(lefts, rights)


def solution(mesh):
    placed = (
        P(("row", "col"), None),
        P(),
        P("row", "col", None),
        P("col", None, None, "row"),
        P("row", "col", None, None, None),
        P("row", "col"),
        P("col"),
        P(("row", "col"), None),
        P(("row", "col"), None),
        P(("row", "col")),
        P(("row", "col")),
    )
    return jax.shard_map(
        per_device,
        mesh=mesh,
        in_specs=placed,
        out_specs=P("row", "col", None, None),
        check_vma=False,
    )
```

```python
import jax
import jax.numpy as jnp
from jax import lax
from jax.experimental import pallas as pl
from jax.experimental.pallas import tpu as pltpu
from jax.sharding import PartitionSpec as P

B = 512
K = 64
TR = 8
TC = 4
NEAR = 256
CAP = 4
RB = 32
N_ROW = 8
N_COL = 16
N_DEV = 128
N_IN = 10
MESH = pl.DeviceIdType.MESH
F32 = jnp.float32
BF16 = jnp.bfloat16
NN = (((1,), (0,)), ((), ()))
NT = (((1,), (1,)), ((), ()))
TN = (((0,), (0,)), ((), ()))


def dot(a, b, dims):
    return lax.dot_general(a, b, dims, preferred_element_type=F32)


def iota(shape, dim):
    return lax.broadcasted_iota(jnp.int32, shape, dim)


def split(a):
    high = a.astype(BF16)
    return high, (a - high.astype(F32)).astype(BF16)


def halves_dot(a, b_high, b_low, dims):
    a_high, a_low = split(a)
    return dot(a_high, b_high, dims) + (dot(a_high, b_low, dims) + dot(a_low, b_high, dims))


def exchange_kernel(near_count, *refs):
    sources, (lefts, rights) = refs[:N_IN], refs[N_IN : N_IN + 2]
    held, local_sems = refs[N_IN + 2 : 2 * N_IN + 1], refs[2 * N_IN + 1]
    near_dest, near_row, near_vals, diag_tile, panel_row, pivot_order, pattern, panel_col, ranks = held
    (
    near_out,
    near_in,
    meta_own,
    meta_row,
    meta_all,
    diag_x,
    diag_all,
    panel_all,
    grid,
    one_send,
    one_recv,
    ring_send,
    ring_recv,
    row_ready,
    ) = refs[2 * N_IN + 2 :]
    loads = [
        pltpu.make_async_copy(source, place, local_sems.at[k])
        for k, (source, place) in enumerate(zip(sources, held))
    ]
    trail = sources[-1]
    loads.append(pltpu.make_async_copy(trail.at[:, :, 0], lefts.at[:, :, pl.ds(0, K)], local_sems.at[N_IN]))
    loads.append(pltpu.make_async_copy(trail.at[:, :, 1], rights.at[:, :, pl.ds(0, K)], local_sems.at[N_IN + 1]))
    for load in loads:
        load.start()

    row = lax.axis_index("row")
    col = lax.axis_index("col")
    y, x = col // 4, lax.rem(col, 4)
    z, core = row // 2, lax.rem(row, 2)
    me = row * N_COL + col
    me_in = col * N_ROW + row

    def up(v):
        return lax.rem(v + 1, 4)

    def down(v):
        return lax.rem(v + 3, 4)

    barrier = pltpu.get_barrier_semaphore()

    row_peers = [(lax.rem(row + k, N_ROW), col) for k in range(1, N_ROW)]
    col_peers = [(row, lax.rem(col + k, N_COL)) for k in range(1, N_COL)]
    for peer in col_peers + row_peers:
        pl.semaphore_signal(barrier, inc=1, device_id=peer, device_id_type=MESH)
    pl.semaphore_wait(barrier, len(col_peers) + len(row_peers))
    for peer in row_peers:
        pl.semaphore_signal(row_ready, inc=1, device_id=peer, device_id_type=MESH)

    def copy(src, dst, sems, device):
        return pltpu.make_async_remote_copy(
            src_ref=src,
            dst_ref=dst,
            send_sem=sems[0],
            recv_sem=sems[1],
            device_id=device,
            device_id_type=MESH,
        )

    for load in loads[:3]:
        load.wait()

    dest_lane = near_dest[...]
    eye = iota((NEAR, NEAR), 0) == iota((NEAR, NEAR), 1)
    dest_col = jnp.sum(jnp.where(eye, dest_lane, 0), axis=1, keepdims=True)
    row_col = jnp.sum(jnp.where(eye, near_row[...], 0), axis=1, keepdims=True)
    earlier = (dest_col == dest_lane) & (iota((NEAR, NEAR), 1) < iota((NEAR, NEAR), 0))
    position = jnp.sum(jnp.where(earlier, 1, 0), axis=1, keepdims=True)
    live = iota((NEAR, 1), 0) < near_count[0]
    slot = jnp.where(live, dest_col * CAP + position, -1)
    placing = slot == iota((NEAR, N_DEV * CAP), 1)
    table = jnp.sum(jnp.where(placing, (row_col + 1).astype(F32), 0.0), axis=0, keepdims=True)
    placed = dot(jnp.where(placing, 1.0, 0.0).astype(BF16), near_vals[...], TN)
    low = iota((64, 8, 128), 1) < 4
    pieces = [placed[:, 128 * b : 128 * b + 128].reshape(64, 8, 128) for b in range(4)]
    turned = [pltpu.roll(p, 4, 1) for p in pieces]
    even = jnp.concatenate(
        [jnp.where(low, pieces[0], turned[1]), jnp.where(low, pieces[2], turned[3])], axis=1
    )
    odd = jnp.concatenate(
        [jnp.where(low, turned[0], pieces[1]), jnp.where(low, turned[2], pieces[3])], axis=1
    )
    both = jnp.concatenate([even[:, None], odd[:, None]], axis=1)
    near_out[...] = both.reshape(N_DEV, 16, 128).astype(BF16)

    meta = jnp.zeros((32, 128), F32)
    for m in range(4):
        meta = meta + jnp.where(
            iota((32, 128), 0) == 4 * row + m, table[:, 128 * m : 128 * m + 128], 0.0
        )
    meta_own[...] = meta.astype(BF16)

    for load in loads[3:9]:
        load.wait()

    own_rows = diag_tile[...]
    diag_x[x] = own_rows
    panel_all[z, core] = panel_row[...]


    ones = iter(range(64))

    def sems():
        k = next(ones)
        return one_send.at[k], one_recv.at[k]

    def finish(copies):
        for c in copies:
            c.wait_recv()

    started = []

    def begin(copies):
        for c in copies:
            c.start()
        started.extend(copies)

    meta_row_copies = []
    for k in range(1, N_ROW):
        meta_row_copies.append(
            copy(meta_own, meta_row.at[k], sems(), (lax.rem(row + k, N_ROW), col))
        )
    begin(meta_row_copies)
    diag_x_copies = [
        copy(diag_x.at[x], diag_x.at[x], sems(), (row, 4 * y + lax.rem(x + k, 4))) for k in (1, 3, 2)
    ]
    begin(diag_x_copies)

    near_sems = sems()

    def send_near(target_row, target_col):
        other = target_row * N_COL + target_col
        copy(near_out.at[other], near_in.at[me_in], near_sems, (target_row, target_col)).start()

    offsets = [
        (dz, dcore, dy, dx)
        for dz in range(4)
        for dcore in range(2)
        for dy in range(4)
        for dx in range(4)
        if (dz, dcore) != (0, 0) and (dy, dx) != (0, 0)
    ]
    hops = [0, 1, 2, 1]
    offsets.sort(key=lambda o: (-hops[o[0]] - hops[o[2]] - hops[o[3]], (7 * o[0] + 5 * o[2] + 3 * o[3] + o[1]) % 8))

    def send_far(some):
        for dz, dcore, dy, dx in some:
            other_core = lax.rem(core + dcore, 2)
            send_near(
                2 * lax.rem(z + dz, 4) + other_core, 4 * lax.rem(y + dy, 4) + lax.rem(x + dx, 4)
            )

    for peer in col_peers + row_peers:
        send_near(*peer)
    pl.semaphore_wait(row_ready, len(row_peers))
    send_far(offsets[:60])

    finish(meta_row_copies)
    total = meta_own[...].astype(F32)
    for k in range(1, N_ROW):
        total = total + meta_row[k].astype(F32)
    meta_all[col] = total.astype(BF16)
    meta_copies = [
        copy(meta_all.at[col], meta_all.at[col], sems(), (row, lax.rem(col + k, N_COL)))
        for k in range(1, N_COL)
    ]
    begin(meta_copies)
    send_far(offsets[60:])
    near_in[me_in] = near_out[me]

    finish(diag_x_copies)
    mine = diag_all.at[z, core, pl.ds(pl.multiple_of(16 * y, 16), 16)]
    mine[...] = jnp.concatenate([diag_x[k] for k in range(4)], axis=0)
    diag_y_copies = [copy(mine, mine, sems(), (row, 4 * lax.rem(y + k, 4) + x)) for k in (1, 3, 2)]
    begin(diag_y_copies)


    finish(meta_copies)
    slots = N_DEV * CAP
    ids = iota((slots, 1), 0)
    wanted = (ids // CAP) * CAP + me // 32
    choose = jnp.where(iota((slots, slots), 1) == wanted, 1.0, 0.0).astype(BF16)
    named = dot(choose, meta_all[...].reshape(slots, 128), NN)
    lane = lax.rem(me, 32) * CAP + lax.rem(ids, CAP)
    target = jnp.sum(jnp.where(iota((slots, 128), 1) == lane, named, 0.0), axis=1, keepdims=True)
    landing = jnp.where(target.astype(jnp.int32) - 1 == iota((slots, 256), 1), 1.0, 0.0).astype(BF16)

    near_all = near_in.at[pl.ds(0, N_DEV - 1)]
    pltpu.make_async_copy(near_all, near_all, near_sems[1]).wait()
    both = near_in[...].astype(F32).reshape(64, 2, 16, 128)
    even, odd = both[:, 0], both[:, 1]
    columns = []
    for b in range(0, 4, 2):
        first, second = even[:, 4 * b : 4 * b + 8], odd[:, 4 * b : 4 * b + 8]
        columns.append(jnp.where(low, first, pltpu.roll(second, 4, 1)).reshape(slots, 128))
        columns.append(jnp.where(low, pltpu.roll(first, 4, 1), second).reshape(slots, 128))
    arrived = jnp.concatenate(columns, axis=1).astype(BF16)
    additions = dot(landing, arrived, TN)
    corrected = (panel_col[...].astype(F32) + additions.reshape(TR, RB, B)).astype(BF16)

    def ring_copy(i, phase, k, part, device):
        return copy(part, part, (ring_send.at[i, phase, k], ring_recv.at[i, phase, k]), device)

    def first_phase(i):
        if i % 2 == 0:
            plus, minus = (row, 4 * y + up(x)), (row, 4 * y + down(x))
            before, after = grid.at[i, y, down(x)], grid.at[i, y, up(x)]
        else:
            plus, minus = (row, 4 * up(y) + x), (row, 4 * down(y) + x)
            before, after = grid.at[i, down(y), x], grid.at[i, up(y), x]
        own = grid.at[i, y, x]
        return (
            ring_copy(i, 0, 0, own, plus),
            ring_copy(i, 0, 1, own, minus),
            ring_copy(i, 0, 2, before.at[pl.ds(0, 16)], plus),
            ring_copy(i, 0, 3, after.at[pl.ds(16, 16)], minus),
        )

    def second_phase(i):
        if i % 2 == 0:
            plus, minus = (row, 4 * up(y) + x), (row, 4 * down(y) + x)
            own = grid.at[i, y]
            before, after = grid.at[i, down(y), pl.ds(0, 2)], grid.at[i, up(y), pl.ds(2, 2)]
        else:
            plus, minus = (row, 4 * y + up(x)), (row, 4 * y + down(x))
            own = grid.at[i, :, x]
            before, after = grid.at[i, pl.ds(0, 2), down(x)], grid.at[i, pl.ds(2, 2), up(x)]
        return (
            ring_copy(i, 1, 0, own, plus),
            ring_copy(i, 1, 1, own, minus),
            ring_copy(i, 1, 2, before, plus),
            ring_copy(i, 1, 3, after, minus),
        )

    one = [first_phase(i) for i in range(TR)]
    two = [second_phase(i) for i in range(TR)]
    for i in range(TR):
        grid[i, y, x] = corrected[i]
        begin(one[i][:2])
    panel_z_copies = [
        copy(
            panel_all.at[z, core],
            panel_all.at[z, core],
            sems(),
            (2 * lax.rem(z + k, 4) + core, col),
        )
        for k in (1, 3, 2)
    ]
    begin(panel_z_copies)


    for i in range(TR):
        one[i][0].wait_recv()
        begin([one[i][2]])
        one[i][1].wait_recv()
        begin([one[i][3]])
    finish(diag_y_copies)
    diag_z_copies = [
        copy(
            diag_all.at[z, core],
            diag_all.at[z, core],
            sems(),
            (2 * lax.rem(z + k, 4) + core, col),
        )
        for k in (1, 3, 2)
    ]
    begin(diag_z_copies)


    for i in range(TR):
        finish(one[i][2:])
        begin(two[i][:2])

    for i in range(0, 4):
        two[i][0].wait_recv()
        begin([two[i][2]])
        two[i][1].wait_recv()
        begin([two[i][3]])
    finish(panel_z_copies + diag_z_copies)
    partner = (2 * z + 1 - core, col)
    core_copies = [
        copy(diag_all.at[:, core], diag_all.at[:, core], sems(), partner),
        copy(panel_all.at[:, core], panel_all.at[:, core], sems(), partner),
    ]
    begin(core_copies)

    wide_eye = iota((B, B), 0) == iota((B, B), 1)
    pivot_col = jnp.sum(jnp.where(wide_eye, pivot_order[...], 0), axis=1, keepdims=True)
    pivoting = jnp.where(pivot_col == iota((B, B), 1), 1.0, 0.0).astype(BF16)

    for i in range(4, 6):
        two[i][0].wait_recv()
        begin([two[i][2]])
        two[i][1].wait_recv()
        begin([two[i][3]])
    finish(core_copies)
    tile = diag_all[...].reshape(B, B)
    high, low_part = split(tile)
    pivot_high = dot(pivoting, high, NN)
    pivot_low = dot(pivoting, low_part, NN)
    scale = 1.0 / jnp.sum(jnp.where(wide_eye, pivot_high + pivot_low, 0.0), axis=0, keepdims=True)
    pivot_high, pivot_low = pivot_high.astype(BF16), pivot_low.astype(BF16)
    left = jnp.concatenate(
        [panel_all[a, b, :, 0].reshape(TC * K, 64) for a in range(4) for b in range(2)], axis=1
    )
    neg_v = -jnp.concatenate(
        [panel_all[a, b, :, 1].reshape(TC * K, 64) for a in range(4) for b in range(2)], axis=1
    )
    lead = dot(left, pivoting, NT)
    kept = jnp.concatenate(
        [jnp.broadcast_to(pattern[:, j : j + 1], (K, 1)) for j in range(TC)], axis=0
    )
    lead = lead * kept.astype(F32)

    def through_pivot(a):
        return halves_dot(a, pivot_high, pivot_low, NT)

    def once(a):
        scaled = a * scale
        return 2.0 * scaled - through_pivot(scaled) * scale

    inner = once(lead)
    images = (2.0 * inner - once(through_pivot(inner))).astype(BF16)

    for i in range(6, 8):
        two[i][0].wait_recv()
        begin([two[i][2]])
        two[i][1].wait_recv()
        begin([two[i][3]])

    for load in loads[9:]:
        load.wait()
    for i in range(TR):
        for j in range(TC):
            kept = iota((K, B), 0) < ranks[j : j + 1, i : i + 1]
            lefts[i, j, 0:K] = jnp.where(kept, lefts[i, j, 0:K], jnp.zeros((), BF16))
            rights[i, j, K : 2 * K] = neg_v[K * j : K * j + K]

    late = [c for copies in two for c in copies]
    for c in started:
        if not any(c is other for other in late):
            c.wait_send()
    pltpu.make_async_copy(near_all, near_all, near_sems[0]).wait()

    for i in range(TR):
        for c in two[i][:2]:
            c.wait_send()
        finish(two[i][2:])
        product = dot(images, grid[i].reshape(B, B), NT).astype(BF16)
        for j in range(TC):
            lefts[i, j, K : 2 * K] = product[K * j : K * j + K]
        for c in two[i][2:]:
            c.wait_send()


def exchange(near_count, *operands):
    vmem = pl.BlockSpec(memory_space=pltpu.VMEM)
    hbm = pl.BlockSpec(memory_space=pltpu.HBM)
    dma = pltpu.SemaphoreType.DMA
    return pl.pallas_call(
        exchange_kernel,
        out_shape=(
            jax.ShapeDtypeStruct((TR, TC, 2 * K, B), BF16),
            jax.ShapeDtypeStruct((TR, TC, 2 * K, B), BF16),
        ),
        in_specs=[pl.BlockSpec(memory_space=pltpu.SMEM)] + [hbm] * N_IN,
        out_specs=(vmem, vmem),
        scratch_shapes=[
            *[pltpu.VMEM(a.shape, a.dtype) for a in operands[:-1]],
            dma((N_IN + 2,)),
            pltpu.VMEM((N_DEV, 16, 128), BF16),
            pltpu.VMEM((N_DEV, 16, 128), BF16),
            pltpu.VMEM((32, 128), BF16),
            pltpu.VMEM((8, 32, 128), BF16),
            pltpu.VMEM((16, 32, 128), BF16),
            pltpu.VMEM((4, 4, B), F32),
            pltpu.VMEM((4, 2, 64, B), F32),
            pltpu.VMEM((4, 2, TC, 2, K, 64), BF16),
            pltpu.VMEM((TR, 4, 4, RB, B), BF16),
            dma((48,)),
            dma((48,)),
            dma((TR, 2, 4)),
            dma((TR, 2, 4)),
            pltpu.SemaphoreType.REGULAR,
        ],
        compiler_params=pltpu.CompilerParams(
            collective_id=0, has_side_effects=True, vmem_limit_bytes=28 << 20
        ),
    )(near_count, *[pltpu.with_memory_space_constraint(a, pltpu.HBM) for a in operands])


def update_kernel(lefts, rights, out, made, sems):
    copies = []
    for i in range(TR):
        for j in range(TC):
            made[i, j] = dot(lefts[i, j], rights[i, j], TN).astype(BF16)
            copies.append(pltpu.make_async_copy(made.at[i, j], out.at[i, j], sems.at[i, j]))
            copies[-1].start()
    for copy in copies:
        copy.wait()


def update(lefts, rights):
    vmem = pl.BlockSpec(memory_space=pltpu.VMEM)
    return pl.pallas_call(
        update_kernel,
        out_shape=jax.ShapeDtypeStruct((TR, TC, B, B), BF16),
        in_specs=[vmem, vmem],
        out_specs=pl.BlockSpec(memory_space=pltpu.HBM),
        scratch_shapes=[
            pltpu.VMEM((TR, TC, B, B), BF16),
            pltpu.SemaphoreType.DMA((TR, TC)),
        ],
        compiler_params=pltpu.CompilerParams(vmem_limit_bytes=30 << 20),
    )(lefts, rights)


def per_device(
    diag_tile,
    pivot_order,
    panel_col,
    panel_row,
    trail_factors,
    tile_ranks,
    pattern,
    near_vals,
    near_dest,
    near_row,
    near_count,
):
    lefts, rights = exchange(
        near_count,
        near_dest.reshape(1, NEAR),
        near_row.reshape(1, NEAR),
        near_vals,
        diag_tile,
        panel_row,
        pivot_order.reshape(1, B),
        pattern.reshape(1, TC),
        panel_col,
        tile_ranks.T,
        trail_factors,
    )
    return update(lefts, rights)


def solution(mesh):
    placed = (
        P(("row", "col"), None),
        P(),
        P("row", "col", None),
        P("col", None, None, "row"),
        P("row", "col", None, None, None),
        P("row", "col"),
        P("col"),
        P(("row", "col"), None),
        P(("row", "col"), None),
        P(("row", "col")),
        P(("row", "col")),
    )
    return jax.shard_map(
        per_device,
        mesh=mesh,
        in_specs=placed,
        out_specs=P("row", "col", None, None),
        check_vma=False,
    )
```
